1024 devices in a mesh: row: 8 (over x, z_hi), col: 128 (over y, z_lo, core).
Axes of the slice: x: 4, y: 4, z: 32 (z_hi: 2, z_lo: 16; z = z_hi * 16 + z_lo), core: 2. Of those that a mesh axis runs over, the one named last changes fastest.
Arguments:
- amplitudes: bfloat16 [1024, 16384], P('row', 'col'), may hold values from -6 to 6
- amp_kept: int32 [8, 128], P('row', 'col'), may hold values 0 or 1
- own_tiles: bfloat16 [20480, 128, 128], P('col'), may hold values from -0.15625 to 0.15625
- own_k: int32 [20480], P('col'), may hold values from 0 to 127
- own_out: int32 [20480], P('col'), may hold values from 0 to 3
- own_live: int32 [20480], P('col'), may hold values from 0 to 1, as said below
- help_tiles: bfloat16 [4096, 128, 128], P('col'), may hold values from -0.15625 to 0.15625
- help_k: int32 [4096], P('col'), may hold values from 0 to 127
- help_out: int32 [4096], P('col'), may hold values from 0 to 3
- help_live: int32 [4096], P('col'), may hold values from 0 to 1, as said below
Outputs:
- ladder: bfloat16 [1024, 65536], P('row', 'col')
The draws below stay inside these ranges and needn't reach their ends.
Inputs may be any that keep to these rules, and one draw needn't show every extreme that they name: `own_live`: live own slots of an index of col come first. Of the two indices c and c + 64, one is busy with 120 or more live own slots, the other has 40 to 80; one busy index has all 160 live in every draw. `help_live`: live handed slots come first. A busy index of col has 16 or more live, one busy index all 32 in every draw; the other index of its pair has at most 8.
All inputs are finite; a program needn't handle non-finite values. No bound on the sum of `amp_kept` on one device may be relied on, other than what follows from the above.
Results may differ from the reference program's by a relative error of at most 0.011.
Values may be sent and summed in bfloat16 or wider, within the bound.
No kernel may reach another device: no remote copies, remote signals or barrier semaphores. Data moves between devices by JAX's collectives and lax.ppermute only.
A program may use at most 32 MiB of HBM per device.

```python
import jax
import jax.numpy as jnp
from jax import lax

TILE = 128
OB = 4
OWN = 160
HELP = 32
KT = 128
ROWS = 1024
OUTCOLS = 65536
N_ROW = 8
N_COL = 128


def pair_layout(key):
    half = N_COL // 2
    busy_first = jax.random.randint(jax.random.fold_in(key, 101), (half,), 0, 2)
    chosen = jax.random.randint(jax.random.fold_in(key, 102), (), 0, N_COL)
    index = jnp.arange(N_COL)
    pair = index % half
    first_side = (index < half).astype(jnp.int32)
    busy = busy_first[pair] == first_side
    busy = jnp.where(pair == chosen % half, index == chosen, busy)
    return (busy, chosen)


def live_slots(counts, slots):
    live = jnp.arange(slots)[None, :] < counts[:, None]
    return live.astype(jnp.int32).reshape(-1)


def draw_own_live(key, part):
    busy, chosen = pair_layout(key)
    key = jax.random.fold_in(key, 11)
    heavy = jax.random.randint(key, (N_COL,), 3 * OWN // 4, OWN + 1)
    light = jax.random.randint(jax.random.fold_in(key, 5), (N_COL,), OWN // 4, OWN // 2 + 1)
    counts = jnp.where(busy, heavy, light)
    counts = jnp.where(jnp.arange(N_COL) == chosen, OWN, counts)
    return live_slots(counts, OWN)


def draw_help_live(key, part):
    busy, chosen = pair_layout(key)
    key = jax.random.fold_in(key, 23)
    heavy = jax.random.randint(key, (N_COL,), HELP // 2, HELP + 1)
    light = jax.random.randint(jax.random.fold_in(key, 5), (N_COL,), 0, HELP // 4 + 1)
    counts = jnp.where(busy, heavy, light)
    counts = jnp.where(jnp.arange(N_COL) == chosen, HELP, counts)
    return live_slots(counts, HELP)


def plant(values, rng, low, high):
    place = [jax.random.randint(jax.random.fold_in(rng, axis), (), 0, length) for axis, length in enumerate(values.shape)]
    main_axis = values.shape.index(max(values.shape))
    next_to = place[:main_axis] + [(place[main_axis] + 1) % values.shape[main_axis]] + place[main_axis + 1:]
    return values.at[tuple(place)].set(low).at[tuple(next_to)].set(high)


def block_levels(rng, shape, split, least, top_value):
    def one(position, shards_of):
        draws = jax.random.uniform(jax.random.fold_in(jax.random.fold_in(rng, 6), position), (shards_of,), jnp.float32, least / len(split), top_value / len(split))
        return jnp.repeat(jnp.exp(draws), shape[position] // shards_of).reshape((-1,) + (1,) * (len(shape) - position - 1))

    level = one(*split[0])
    for cut in split[1:]:
        level = level * one(*cut)
    return level


def gaussian(rng, extent, deviation, bound, pieces=(), kind=jnp.bfloat16):
    values = jax.random.normal(rng, extent, jnp.float32) * deviation
    if len(pieces) > 0:
        values = block_levels(rng, extent, pieces, -0.22, 0.18) * values
    return jnp.clip(values, min=-bound, max=bound).astype(kind)


def setup_inputs(seed: int = 0) -> dict:
    splits = jax.random.split(jax.random.key(seed), 11)
    amplitudes = gaussian(splits[0], (ROWS, KT * TILE), 1.0, 6.0, ((0, 8), (1, 128)))
    amp_kept = plant((jax.random.randint(splits[1], (N_ROW, KT), 0, 4) < 1).astype(jnp.int32), jax.random.fold_in(splits[1], 1), 0, 1)
    own_tiles = gaussian(splits[2], (N_COL * OWN, TILE, TILE), (TILE * OWN // (4 * OB)) ** -0.5, 0.15625, ((0, 128),))
    own_k = plant(jax.random.randint(splits[3], (N_COL * OWN,), 0, KT), jax.random.fold_in(splits[3], 1), 0, KT - 1).astype(jnp.int32)
    own_out = plant(jax.random.randint(splits[4], (N_COL * OWN,), 0, OB), jax.random.fold_in(splits[4], 1), 0, OB - 1).astype(jnp.int32)
    own_live = draw_own_live(jax.random.fold_in(splits[10], 71), 0)
    help_tiles = gaussian(splits[6], (N_COL * HELP, TILE, TILE), (TILE * OWN // (4 * OB)) ** -0.5, 0.15625, ((0, 128),))
    help_k = plant(jax.random.randint(splits[7], (N_COL * HELP,), 0, KT), jax.random.fold_in(splits[7], 1), 0, KT - 1).astype(jnp.int32)
    help_out = plant(jax.random.randint(splits[8], (N_COL * HELP,), 0, OB), jax.random.fold_in(splits[8], 1), 0, OB - 1).astype(jnp.int32)
    help_live = draw_help_live(jax.random.fold_in(splits[10], 71), 0)
    return {"amplitudes": amplitudes, "amp_kept": amp_kept, "own_tiles": own_tiles, "own_k": own_k, "own_out": own_out, "own_live": own_live, "help_tiles": help_tiles, "help_k": help_k, "help_out": help_out, "help_live": help_live}


def owner_terms(blocks, tiles, kinds, outs, live):
    picked = jnp.take(blocks, kinds, axis=1).astype(jnp.float32)
    prod = jnp.einsum("rtk,tkc->rtc", picked, tiles.astype(jnp.float32))
    weights = (outs[:, None] == jnp.arange(OB, dtype=jnp.int32)[None, :]).astype(jnp.float32) * live[:, None].astype(jnp.float32)
    return jnp.einsum("rtc,to->roc", prod, weights)


def reference(amplitudes, amp_kept, own_tiles, own_k, own_out, own_live, help_tiles, help_k, help_out, help_live):
    kept_full = jnp.repeat(jnp.repeat(amp_kept, TILE, axis=0), TILE, axis=1).astype(jnp.bfloat16)
    kept_amps = amplitudes * kept_full
    blocks = kept_amps.reshape(ROWS, KT, TILE)
    own_tiles = own_tiles.reshape(N_COL, OWN, TILE, TILE)
    help_tiles = help_tiles.reshape(N_COL, HELP, TILE, TILE)

    def per_owner(items):
        own_sum = owner_terms(blocks, items[0], items[1], items[2], items[3])
        help_sum = owner_terms(blocks, items[4], items[5], items[6], items[7])
        return (own_sum + help_sum).astype(jnp.bfloat16)

    result = lax.map(per_owner, (own_tiles, own_k.reshape(N_COL, OWN), own_out.reshape(N_COL, OWN), own_live.reshape(N_COL, OWN), help_tiles, help_k.reshape(N_COL, HELP), help_out.reshape(N_COL, HELP), help_live.reshape(N_COL, HELP)))
    return jnp.transpose(result, (1, 0, 2, 3)).reshape(ROWS, OUTCOLS)
```

```python
import functools

import jax
import jax.numpy as jnp
import numpy as np
from jax import lax
from jax.experimental import pallas as pl
from jax.experimental.pallas import tpu as pltpu
from jax.sharding import PartitionSpec as P

TILE = 128
OB = 4
NY, NZH, NZL, NC = 4, 4, 4, 2
LINE = NZH * NZL
WIDE = 4
OWN_CHUNK = 16


def split_col(i):
    return i // (LINE * NC), (i // (NZL * NC)) % NZH, (i // NC) % NZL, i % NC


def join_col(y, zh, zl, c):
    return ((y * NZH + zh) * NZL + zl) * NC + c


def shift(dy=0, dzh=0, dzl=0, dc=0):
    pairs = []
    for i in range(NY * LINE * NC):
        y, zh, zl, c = split_col(i)
        j = join_col((y + dy) % NY, (zh + dzh) % NZH, (zl + dzl) % NZL, (c + dc) % NC)
        pairs.append((i, j))
    return pairs


def move(x, **d):
    return lax.ppermute(x, "col", shift(**d))


def prep_kernel(slots_own, slots_help, own_k, own_out, own_live, help_k, help_out, help_live,
                table, lists, counts):
    del slots_own, slots_help
    cap = lists.shape[0] // 3

    def scan(n, ks, outs, live, base, ns):
        def step(s, ns):
            code = table[ks[s]]
            phase, local = code // 64, code % 64
            entry = ((s + base) * 64 + local) * 8 + outs[s]
            on = live[s]
            new = []
            for p in range(3):
                hit = jnp.where(phase == p, on, 0)
                lists[p * cap + ns[p]] = entry
                new.append(ns[p] + hit)
            return tuple(new)

        return lax.fori_loop(0, n, step, ns)

    n_own, n_help = own_k.shape[0], help_k.shape[0]
    ns = scan(n_own, own_k, own_out, own_live, 0, (0, 0, 0))
    ns = scan(n_help, help_k, help_out, help_live, n_own, ns)
    for p in range(3):
        counts[p] = ns[p]
        for w in range(WIDE):
            lists[p * cap + ns[p] + w] = OB


def task_kernel(phase, cap, last, lists, counts, own_tiles, help_tiles, acc_in, *rest):
    n_pieces = len(rest) - 7
    pieces, out = rest[:n_pieces], rest[n_pieces]
    amps, tiles, acc, own_sems, help_sem, amp_sems = rest[n_pieces + 1:]
    n_own = own_tiles.shape[0]
    copies = []
    for j, piece in enumerate(pieces):
        copies.append(pltpu.make_async_copy(piece, amps.at[pl.ds(j * LINE, LINE)], amp_sems.at[j]))
    for j in range(n_own // OWN_CHUNK):
        part = pl.ds(j * OWN_CHUNK, OWN_CHUNK)
        copies.append(pltpu.make_async_copy(own_tiles.at[part], tiles.at[part], own_sems.at[j]))
    copies.append(pltpu.make_async_copy(
        help_tiles, tiles.at[pl.ds(n_own, help_tiles.shape[0])], help_sem.at[0]))
    for copy in copies:
        copy.start()
    acc[pl.ds(0, OB)] = acc_in[...]
    for copy in copies:
        copy.wait()

    def step(g, carry):
        outs, prods = [], []
        for w in range(WIDE):
            entry = lists[phase * cap + g * WIDE + w]
            outs.append(entry % 8)
            a = amps[(entry // 8) % 64]
            b = tiles[entry // 512]
            prods.append(jnp.dot(a, b, preferred_element_type=jnp.float32))
        for w in range(WIDE):
            acc[outs[w]] += prods[w]
        return carry

    lax.fori_loop(0, (counts[phase] + WIDE - 1) // WIDE, step, 0)
    if last:
        for o in range(OB):
            out[:, o * TILE:(o + 1) * TILE] = acc[o].astype(out.dtype)
    else:
        out[...] = acc[pl.ds(0, OB)]


def run_tasks(phase, lists, counts, own_tiles, help_tiles, acc_in, pieces, last):
    n_own, n_help = own_tiles.shape[0], help_tiles.shape[0]
    n = n_own + n_help
    cap = lists.shape[0] // 3
    if last:
        out_shape = jax.ShapeDtypeStruct((TILE, OB * TILE), jnp.bfloat16)
    else:
        out_shape = jax.ShapeDtypeStruct((OB, TILE, TILE), jnp.float32)
    anywhere = pl.BlockSpec(memory_space=pl.ANY)
    smem = pl.BlockSpec(memory_space=pltpu.SMEM)
    vmem = pl.BlockSpec(memory_space=pltpu.VMEM)
    return pl.pallas_call(
        functools.partial(task_kernel, phase, cap, last),
        out_shape=out_shape,
        in_specs=[smem, smem, anywhere, anywhere, vmem] + [anywhere] * len(pieces),
        out_specs=vmem,
        scratch_shapes=[
            pltpu.VMEM((len(pieces) * LINE, TILE, TILE), jnp.bfloat16),
            pltpu.VMEM((n, TILE, TILE), jnp.bfloat16),
            pltpu.VMEM((OB + 1, TILE, TILE), jnp.float32),
            pltpu.SemaphoreType.DMA((n_own // OWN_CHUNK,)),
            pltpu.SemaphoreType.DMA((1,)),
            pltpu.SemaphoreType.DMA((len(pieces),)),
        ],
        compiler_params=pltpu.CompilerParams(vmem_limit_bytes=24 << 20),
        cost_estimate=pl.CostEstimate(flops=n // 3 * 2 * TILE ** 3, bytes_accessed=8 << 20, transcendentals=0),
        name=f"tasks{phase}",
    )(lists, counts, own_tiles, help_tiles, acc_in, *pieces)


def prepare(own_k, own_out, own_live, help_k, help_out, help_live):
    me = lax.axis_index("col")
    y, zh, zl, c = split_col(me)
    ky, kzh, kzl, kc = split_col(jnp.arange(NY * LINE * NC, dtype=jnp.int32))
    dy, dzh, dzl, dc = (y - ky) % NY, (zh - kzh) % NZH, (zl - kzl) % NZL, (c - kc) % NC
    near = dzl * NZH + dzh
    local = jnp.where(dy == 0, dc, dy - 1) * LINE + near
    phase = jnp.where(dy == 0, 0, 1 + dc)
    table = phase * 64 + local
    n = own_k.shape[0] + help_k.shape[0]
    smem = pl.BlockSpec(memory_space=pltpu.SMEM)
    args = (own_k, own_out, own_live, help_k, help_out, help_live, table)

    def kernel(*refs):
        prep_kernel(None, None, *refs)

    return pl.pallas_call(
        kernel,
        out_shape=(jax.ShapeDtypeStruct((3 * (n + 8),), jnp.int32), jax.ShapeDtypeStruct((8,), jnp.int32)),
        in_specs=[smem] * len(args),
        out_specs=(smem, smem),
        name="prep",
        cost_estimate=pl.CostEstimate(flops=0, bytes_accessed=8 << 20, transcendentals=0),
    )(*args)


def shards(
    amplitudes,
    amp_kept,
    own_tiles,
    own_k,
    own_out,
    own_live,
    help_tiles,
    help_k,
    help_out,
    help_live,
):
    kept = amplitudes * amp_kept.astype(jnp.bfloat16)
    lists, counts = prepare(own_k, own_out, own_live, help_k, help_out, help_live)
    first = jnp.stack([kept] + [move(kept, dzh=k) for k in (1, 2, 3)])
    line = jnp.concatenate([first] + [move(first, dzl=k) for k in (1, 2, 3)])
    ys = {k: move(line, dy=k) for k in (1, 3, 2)}
    line_c = move(line, dc=1)
    ys_c = {k: move(ys[k], dc=1) for k in (1, 3, 2)}
    tasks = functools.partial(run_tasks, lists=lists, counts=counts, own_tiles=own_tiles, help_tiles=help_tiles)
    acc = jnp.zeros((OB, TILE, TILE), jnp.float32)
    acc = tasks(0, acc_in=acc, pieces=[line, line_c], last=False)
    acc = tasks(1, acc_in=acc, pieces=[ys[1], ys[2], ys[3]], last=False)
    return tasks(2, acc_in=acc, pieces=[ys_c[1], ys_c[2], ys_c[3]], last=True)


def solution(mesh):
    return jax.shard_map(
        shards,
        mesh=mesh,
        in_specs=(
            P("row", "col"),
            P("row", "col"),
            P("col", None, None),
            P("col"),
            P("col"),
            P("col"),
            P("col", None, None),
            P("col"),
            P("col"),
            P("col"),
        ),
        out_specs=P("row", "col"),
        check_vma=False,
    )
```

```python
import functools

import jax
import jax.numpy as jnp
import numpy as np
from jax import lax
from jax.experimental import pallas as pl
from jax.experimental.pallas import tpu as pltpu
from jax.sharding import PartitionSpec as P

TILE = 128
OB = 4
NY, NZH, NZL, NC = 4, 4, 4, 2
LINE = NZH * NZL
PIECES = NC * NY
WIDE = 4


def split_col(i):
    return i // (LINE * NC), (i // (NZL * NC)) % NZH, (i // NC) % NZL, i % NC


def join_col(y, zh, zl, c):
    return ((y * NZH + zh) * NZL + zl) * NC + c


def shift(dy=0, dzh=0, dzl=0, dc=0):
    pairs = []
    for i in range(NY * LINE * NC):
        y, zh, zl, c = split_col(i)
        j = join_col((y + dy) % NY, (zh + dzh) % NZH, (zl + dzl) % NZL, (c + dc) % NC)
        pairs.append((i, j))
    return pairs


def move(x, **d):
    return lax.ppermute(x, "col", shift(**d))


def prep_kernel(own_k, own_out, own_live, help_k, help_out, help_live, table, own_tiles, help_tiles,
                lists, counts, tiles, sems, *held):
    n_own, n_help = own_k.shape[0], help_k.shape[0]
    cap = lists.shape[0] // PIECES
    loads = []
    for j, ref in enumerate((own_k, own_out, own_live, help_k, help_out, help_live, table)):
        loads.append(pltpu.make_async_copy(ref, held[j], sems.at[2 + j]))
        loads[j].start()
    own_k, own_out, own_live, help_k, help_out, help_live, table = held
    fetch_own = pltpu.make_async_copy(own_tiles, tiles.at[pl.ds(0, n_own)], sems.at[0])
    fetch_help = pltpu.make_async_copy(help_tiles, tiles.at[pl.ds(n_own, n_help)], sems.at[1])
    fetch_own.start()
    fetch_help.start()
    for p in range(PIECES):
        counts[p] = 0
    for load in loads:
        load.wait()

    def scan(ks, outs, live, base):
        def step(s, carry):
            code = table[ks[s]]
            p = code // LINE
            n = counts[p]
            lists[p * cap + n] = ((s + base) * LINE + code % LINE) * 8 + outs[s]
            counts[p] = n + live[s]
            return carry

        lax.fori_loop(0, ks.shape[0], step, 0)

    scan(own_k, own_out, own_live, 0)
    scan(help_k, help_out, help_live, n_own)
    for p in range(PIECES):
        for w in range(WIDE):
            lists[p * cap + counts[p] + w] = OB
    fetch_own.wait()
    fetch_help.wait()


def task_kernel(ids, last, lists, counts, tiles, acc_in, *rest):
    pieces, out, acc = rest[:len(ids)], rest[-2], rest[-1]
    cap = lists.shape[0] // PIECES
    acc[pl.ds(0, OB)] = acc_in[...]
    for p, amps in zip(ids, pieces):

        def step(g, carry, p=p, amps=amps):
            outs, prods = [], []
            for w in range(WIDE):
                entry = lists[p * cap + g * WIDE + w]
                outs.append(entry % 8)
                a = amps[(entry // 8) % LINE]
                b = tiles[entry // (8 * LINE)]
                prods.append(jnp.dot(a, b, preferred_element_type=jnp.float32))
            for w in range(WIDE):
                acc[outs[w]] += prods[w]
            return carry

        lax.fori_loop(0, (counts[p] + WIDE - 1) // WIDE, step, 0)
    if last:
        for o in range(OB):
            out[:, o * TILE:(o + 1) * TILE] = acc[o].astype(out.dtype)
    else:
        out[...] = acc[pl.ds(0, OB)]


def run_tasks(ids, pieces, acc_in, last, lists, counts, tiles):
    if last:
        out_shape = jax.ShapeDtypeStruct((TILE, OB * TILE), jnp.bfloat16)
    else:
        out_shape = jax.ShapeDtypeStruct((OB, TILE, TILE), jnp.float32)
    smem = pl.BlockSpec(memory_space=pltpu.SMEM)
    vmem = pl.BlockSpec(memory_space=pltpu.VMEM)
    n = tiles.shape[0] * len(ids) // PIECES
    return pl.pallas_call(
        functools.partial(task_kernel, ids, last),
        out_shape=out_shape,
        in_specs=[smem, smem, vmem, vmem] + [vmem] * len(pieces),
        out_specs=vmem,
        scratch_shapes=[pltpu.VMEM((OB + 1, TILE, TILE), jnp.float32)],
        compiler_params=pltpu.CompilerParams(vmem_limit_bytes=24 << 20),
        cost_estimate=pl.CostEstimate(flops=n * 20 * TILE ** 3, bytes_accessed=8 << 20, transcendentals=0),
        name="tasks" + "".join(str(p) for p in ids),
    )(lists, counts, tiles, acc_in, *pieces)


def prepare(own_tiles, own_k, own_out, own_live, help_tiles, help_k, help_out, help_live):
    me = lax.axis_index("col")
    y, zh, zl, c = split_col(me)
    ky, kzh, kzl, kc = split_col(jnp.arange(NY * LINE * NC, dtype=jnp.int32))
    dy, dzh, dzl, dc = (y - ky) % NY, (zh - kzh) % NZH, (zl - kzl) % NZL, (c - kc) % NC
    table = ((dc * NY + dy) * NZL + dzl) * NZH + dzh
    n = own_k.shape[0] + help_k.shape[0]
    smem = pl.BlockSpec(memory_space=pltpu.SMEM)
    hbm = pl.BlockSpec(memory_space=pltpu.HBM)
    scalars = (own_k, own_out, own_live, help_k, help_out, help_live, table)
    return pl.pallas_call(
        prep_kernel,
        out_shape=(
            jax.ShapeDtypeStruct((PIECES * (n + 8),), jnp.int32),
            jax.ShapeDtypeStruct((PIECES,), jnp.int32),
            pltpu.VMEM((n, TILE, TILE), jnp.bfloat16),
        ),
        in_specs=[hbm] * 9,
        out_specs=(smem, smem, pl.BlockSpec(memory_space=pltpu.VMEM)),
        scratch_shapes=[pltpu.SemaphoreType.DMA((2 + len(scalars),))]
        + [pltpu.SMEM(v.shape, jnp.int32) for v in scalars],
        name="prep",
        compiler_params=pltpu.CompilerParams(vmem_limit_bytes=24 << 20),
        cost_estimate=pl.CostEstimate(flops=0, bytes_accessed=8 << 20, transcendentals=0),
    )(*[pltpu.with_memory_space_constraint(v, pltpu.HBM) for v in (*scalars, own_tiles, help_tiles)])


def shards(
    amplitudes,
    amp_kept,
    own_tiles,
    own_k,
    own_out,
    own_live,
    help_tiles,
    help_k,
    help_out,
    help_live,
):
    kept = amplitudes * amp_kept.astype(jnp.bfloat16)
    far = [kept] + [move(kept, dzh=k) for k in (1, 2, 3)]
    lists, counts, tiles = prepare(
        own_tiles, own_k, own_out, own_live, help_tiles, help_k, help_out, help_live)
    first = jnp.stack(far)
    line = jnp.concatenate([first] + [move(first, dzl=k) for k in (1, 2, 3)])
    ys = {k: move(line, dy=k) for k in (1, 3, 2)}
    line_c = move(line, dc=1)
    tasks = functools.partial(run_tasks, lists=lists, counts=counts, tiles=tiles)
    acc = jnp.zeros((OB, TILE, TILE), jnp.float32)
    acc = tasks((0, NY), [line, line_c], acc, False)
    ys[1], acc = lax.optimization_barrier((ys[1], acc))
    ys_c = {k: move(ys[k], dc=1) for k in (1, 3, 2)}
    acc = tasks((1, 3, 2), [ys[1], ys[3], ys[2]], acc, False)
    return tasks((NY + 1, NY + 3, NY + 2), [ys_c[1], ys_c[3], ys_c[2]], acc, True)


def solution(mesh):
    return jax.shard_map(
        shards,
        mesh=mesh,
        in_specs=(
            P("row", "col"),
            P("row", "col"),
            P("col", None, None),
            P("col"),
            P("col"),
            P("col"),
            P("col", None, None),
            P("col"),
            P("col"),
            P("col"),
        ),
        out_specs=P("row", "col"),
        check_vma=False,
    )
```

```python
import functools

import jax
import jax.numpy as jnp
import numpy as np
from jax import lax
from jax.experimental import pallas as pl
from jax.experimental.pallas import tpu as pltpu
from jax.sharding import PartitionSpec as P

TILE = 128
OB = 4
NY, NZH, NZL, NC = 4, 4, 4, 2
COLS = NY * NZH * NZL * NC
LINE = NZH * NZL
PIECES = NC * NY
WIDE = 4
PACK = 10
REST = LINE - PACK
META = 16
ABSENT, LATER = 99, 50


def move(x, y=0, zh=0, zl=0, c=0):
    mask = ((y * NZH + zh) * NZL + zl) * NC + c
    return lax.ppermute(x, "col", [(i, i ^ mask) for i in range(COLS)])


def prep_kernel(own_k, own_out, own_live, help_k, help_out, help_live, table, own_tiles, help_tiles,
                lists, counts, tiles, sems, *held):
    n_own, n_help = own_k.shape[0], help_k.shape[0]
    cap = lists.shape[0] // PIECES
    loads = []
    for j, ref in enumerate((own_k, own_out, own_live, help_k, help_out, help_live, table)):
        loads.append(pltpu.make_async_copy(ref, held[j], sems.at[2 + j]))
        loads[j].start()
    own_k, own_out, own_live, help_k, help_out, help_live, table = held
    fetch_own = pltpu.make_async_copy(own_tiles, tiles.at[pl.ds(0, n_own)], sems.at[0])
    fetch_help = pltpu.make_async_copy(help_tiles, tiles.at[pl.ds(n_own, n_help)], sems.at[1])
    fetch_own.start()
    fetch_help.start()
    for p in range(PIECES):
        counts[p] = 0
    for load in loads:
        load.wait()

    def scan(ks, outs, live, base):
        def step(s, carry):
            code = table[ks[s]]
            p = code // LINE
            n = counts[p]
            lists[p * cap + n] = ((s + base) * LINE + code % LINE) * 8 + outs[s]
            counts[p] = n + live[s]
            return carry

        lax.fori_loop(0, ks.shape[0], step, 0)

    scan(own_k, own_out, own_live, 0)
    scan(help_k, help_out, help_live, n_own)
    for p in range(PIECES):
        for w in range(WIDE):
            lists[p * cap + counts[p] + w] = OB
    fetch_own.wait()
    fetch_help.wait()


def pack_kernel(*refs):
    groups, (head, tail) = refs[:NZL], refs[NZL:NZL + 2]
    gone_v, gone_s, sem = refs[NZL + 2:]
    lane = lax.broadcasted_iota(jnp.int32, (8, TILE), 1)
    gone = jnp.zeros((8, TILE), jnp.int32)
    for slot in range(LINE):
        row = groups[slot // NZH][slot % NZH, pl.ds(0, 16), :].astype(jnp.float32)[:1]
        gone = jnp.where((lane == slot) & (row == jnp.inf), 1, gone)
    gone_v[...] = gone
    copy = pltpu.make_async_copy(gone_v, gone_s, sem.at[0])
    copy.start()
    copy.wait()
    lane = lax.broadcasted_iota(jnp.int32, (META, TILE), 1)
    places = jnp.full((META, TILE), ABSENT, jnp.int32)
    n = jnp.int32(0)
    for slot in range(LINE):
        here = gone_s[0, slot] == 0
        tile = groups[slot // NZH].at[slot % NZH]

        @pl.when(here & (n < PACK))
        def _():
            head[pl.ds(pl.multiple_of(n * TILE, TILE), TILE), :] = tile[...]

        @pl.when(here & (n >= PACK))
        def _():
            tail[pl.ds(pl.multiple_of((n - PACK) * TILE, TILE), TILE), :] = tile[...]

        places = jnp.where(lane == slot, jnp.where(here, n, ABSENT), places)
        n = n + jnp.where(here, 1, 0)
    late = (places >= PACK) & (places < ABSENT)
    first = jnp.where(late, LATER, places)
    first = jnp.where(lane == LINE, jnp.where(n > PACK, 1, 0), first)
    second = jnp.where(late, places - PACK, ABSENT)
    second = jnp.where(lane == LINE, 0, second)
    head[pl.ds(PACK * TILE, META), :] = first.astype(jnp.float32).astype(head.dtype)
    tail[pl.ds(REST * TILE, META), :] = second.astype(jnp.float32).astype(tail.dtype)


def pack(groups):
    vmem = pl.BlockSpec(memory_space=pltpu.VMEM)
    return pl.pallas_call(
        pack_kernel,
        out_shape=(
            jax.ShapeDtypeStruct((PACK * TILE + META, TILE), jnp.bfloat16),
            jax.ShapeDtypeStruct((REST * TILE + META, TILE), jnp.bfloat16),
        ),
        in_specs=[vmem] * len(groups),
        out_specs=(vmem, vmem),
        scratch_shapes=[
            pltpu.VMEM((8, TILE), jnp.int32),
            pltpu.SMEM((8, TILE), jnp.int32),
            pltpu.SemaphoreType.DMA((1,)),
        ],
        name="pack",
        compiler_params=pltpu.CompilerParams(vmem_limit_bytes=24 << 20),
    )(*groups)


def task_kernel(ids, places, last, lists, counts, tiles, acc_in, over_in, *rest):
    pieces, rest = rest[:len(ids)], rest[len(ids):]
    outs, (acc, meta_v, meta_s, picked, sem) = rest[:-5], rest[-5:]
    cap = lists.shape[0] // PIECES
    for j, piece in enumerate(pieces):
        meta = piece[pl.ds(places * TILE, META), :].astype(jnp.float32).astype(jnp.int32)
        meta_v[pl.ds(j, 1), :] = meta[:1]
    copy = pltpu.make_async_copy(meta_v, meta_s, sem.at[0])
    copy.start()
    acc[pl.ds(0, OB)] = acc_in[...]
    copy.wait()
    over = over_in[0]
    for j, (p, amps) in enumerate(zip(ids, pieces)):
        over = over + meta_s[j, LINE]

        def pick(e, n, p=p, j=j):
            entry = lists[p * cap + e]
            place = meta_s[j, (entry // 8) % LINE]
            picked[n] = (entry // (8 * LINE)) * (8 * LINE) + place * 8 + entry % 8
            return n + jnp.where(place < places, 1, 0)

        n = lax.fori_loop(0, counts[p], pick, 0)
        for w in range(WIDE):
            picked[n + w] = OB

        def step(g, carry, amps=amps):
            outputs, prods = [], []
            for w in range(WIDE):
                entry = picked[g * WIDE + w]
                outputs.append(entry % 8)
                place = (entry // 8) % LINE
                a = amps[pl.ds(pl.multiple_of(place * TILE, TILE), TILE), :]
                b = tiles[entry // (8 * LINE)]
                prods.append(jnp.dot(a, b, preferred_element_type=jnp.float32))
            for w in range(WIDE):
                acc[outputs[w]] += prods[w]
            return carry

        lax.fori_loop(0, (n + WIDE - 1) // WIDE, step, 0)
    if last:
        for o in range(OB):
            outs[2][:, o * TILE:(o + 1) * TILE] = acc[o].astype(outs[2].dtype)
    outs[0][...] = acc[pl.ds(0, OB)]
    outs[1][0] = over


def run_tasks(ids, pieces, acc_in, last, lists, counts, tiles, places=PACK):
    smem = pl.BlockSpec(memory_space=pltpu.SMEM)
    vmem = pl.BlockSpec(memory_space=pltpu.VMEM)
    out_shape = [jax.ShapeDtypeStruct((OB, TILE, TILE), jnp.float32), jax.ShapeDtypeStruct((1,), jnp.int32)]
    out_specs = [vmem, smem]
    if last:
        out_shape.append(jax.ShapeDtypeStruct((TILE, OB * TILE), jnp.bfloat16))
        out_specs.append(vmem)
    n = tiles.shape[0] * len(ids) // PIECES
    return pl.pallas_call(
        functools.partial(task_kernel, ids, places, last),
        out_shape=out_shape,
        in_specs=[smem, smem, vmem, vmem, smem] + [vmem] * len(pieces),
        out_specs=out_specs,
        scratch_shapes=[
            pltpu.VMEM((OB + 1, TILE, TILE), jnp.float32),
            pltpu.VMEM((8, TILE), jnp.int32),
            pltpu.SMEM((8, TILE), jnp.int32),
            pltpu.SMEM((tiles.shape[0] + 8,), jnp.int32),
            pltpu.SemaphoreType.DMA((1,)),
        ],
        compiler_params=pltpu.CompilerParams(vmem_limit_bytes=24 << 20),
        cost_estimate=pl.CostEstimate(flops=n * 20 * TILE ** 3, bytes_accessed=8 << 20, transcendentals=0),
        name="tasks" + "".join(str(p) for p in ids),
    )(lists, counts, tiles, *acc_in, *pieces)


def prepare(own_tiles, own_k, own_out, own_live, help_tiles, help_k, help_out, help_live):
    apart = lax.axis_index("col") ^ jnp.arange(COLS, dtype=jnp.int32)
    c, zl, zh, y = apart % NC, apart // NC % NZL, apart // (NC * NZL) % NZH, apart // (NC * LINE)
    table = ((c * NY + y) * NZL + zl) * NZH + zh
    n = own_k.shape[0] + help_k.shape[0]
    smem = pl.BlockSpec(memory_space=pltpu.SMEM)
    hbm = pl.BlockSpec(memory_space=pltpu.HBM)
    scalars = (own_k, own_out, own_live, help_k, help_out, help_live, table)
    return pl.pallas_call(
        prep_kernel,
        out_shape=(
            jax.ShapeDtypeStruct((PIECES * (n + 8),), jnp.int32),
            jax.ShapeDtypeStruct((PIECES,), jnp.int32),
            pltpu.VMEM((n, TILE, TILE), jnp.bfloat16),
        ),
        in_specs=[hbm] * 9,
        out_specs=(smem, smem, pl.BlockSpec(memory_space=pltpu.VMEM)),
        scratch_shapes=[pltpu.SemaphoreType.DMA((2 + len(scalars),))]
        + [pltpu.SMEM(v.shape, jnp.int32) for v in scalars],
        name="prep",
        compiler_params=pltpu.CompilerParams(vmem_limit_bytes=24 << 20),
        cost_estimate=pl.CostEstimate(flops=0, bytes_accessed=8 << 20, transcendentals=0),
    )(*[pltpu.with_memory_space_constraint(v, pltpu.HBM) for v in (*scalars, own_tiles, help_tiles)])


def shards(
    amplitudes,
    amp_kept,
    own_tiles,
    own_k,
    own_out,
    own_live,
    help_tiles,
    help_k,
    help_out,
    help_live,
):
    kept = jnp.where(amp_kept != 0, amplitudes * amp_kept.astype(jnp.bfloat16), jnp.inf).astype(jnp.bfloat16)
    first = jnp.stack([kept] + [move(kept, zh=k) for k in (1, 2, 3)])
    head, tail = pack([first] + [move(first, zl=k) for k in (1, 2, 3)])
    lists, counts, tiles = prepare(
        own_tiles, own_k, own_out, own_live, help_tiles, help_k, help_out, help_live)
    tasks = functools.partial(run_tasks, lists=lists, counts=counts, tiles=tiles)
    ys = {k: move(head, y=k) for k in (1, 3, 2)}
    head_c = move(head, c=1)
    acc = (jnp.zeros((OB, TILE, TILE), jnp.float32), jnp.zeros((1,), jnp.int32))
    acc = tasks((0, NY), [head, head_c], acc, False)
    ys[1], acc = lax.optimization_barrier((ys[1], acc))
    ys_c = {k: move(ys[k], c=1) for k in (1, 3, 2)}
    acc = tasks((1, 3, 2), [ys[1], ys[3], ys[2]], acc, False)
    total, over, out = tasks((NY + 1, NY + 3, NY + 2), [ys_c[1], ys_c[3], ys_c[2]], acc, True)

    def second_round(tail, total, over, out):
        line = [tail] + [move(tail, y=k) for k in (1, 2, 3)]
        pieces = line + [move(v, c=1) for v in line]
        return tasks(tuple(range(PIECES)), pieces, (total, over), True, places=REST)[2]

    return lax.cond(over[0] > 0, second_round, lambda tail, total, over, out: out, tail, total, over, out)


def solution(mesh):
    return jax.shard_map(
        shards,
        mesh=mesh,
        in_specs=(
            P("row", "col"),
            P("row", "col"),
            P("col", None, None),
            P("col"),
            P("col"),
            P("col"),
            P("col", None, None),
            P("col"),
            P("col"),
            P("col"),
        ),
        out_specs=P("row", "col"),
        check_vma=False,
    )
```

```python
import functools

import jax
import jax.numpy as jnp
import numpy as np
from jax import lax
from jax.experimental import pallas as pl
from jax.experimental.pallas import tpu as pltpu
from jax.sharding import PartitionSpec as P

TILE = 128
OB = 4
NY, NZH, NZL, NC = 4, 4, 4, 2
COLS = NY * NZH * NZL * NC
LINE = NZH * NZL
PIECES = NC * NY
WIDE = 4
SCAN = 8
PACK = 10
REST = LINE - PACK
META = 16
ABSENT, LATER = 99, 50


def move(x, y=0, zh=0, zl=0, c=0):
    pairs = []
    for i in range(COLS):
        far, near = (i // (NC * NZL) + zh) % NZH, (i // NC + zl) % NZL
        here = ((i // (NC * LINE) ^ y) * NZH + far) * NZL + near
        pairs.append((i, here * NC + (i % NC ^ c)))
    return lax.ppermute(x, "col", pairs)


def prep_kernel(own_k, own_out, own_live, help_k, help_out, help_live, table, own_tiles, help_tiles,
                lists, counts, tiles, sems, *held):
    n_own, n_help = own_k.shape[0], help_k.shape[0]
    cap = lists.shape[0] // PIECES
    loads = []
    for j, ref in enumerate((own_k, own_out, own_live, help_k, help_out, help_live, table)):
        loads.append(pltpu.make_async_copy(ref, held[j], sems.at[2 + j]))
        loads[j].start()
    own_k, own_out, own_live, help_k, help_out, help_live, table = held
    fetch_own = pltpu.make_async_copy(own_tiles, tiles.at[pl.ds(0, n_own)], sems.at[0])
    fetch_help = pltpu.make_async_copy(help_tiles, tiles.at[pl.ds(n_own, n_help)], sems.at[1])
    fetch_own.start()
    fetch_help.start()
    for p in range(PIECES):
        counts[p] = 0
    for load in loads:
        load.wait()

    def scan(ks, outs, live, base):
        def step(s, carry):
            code = table[ks[s]]
            p = code >> 4
            n = counts[p]
            lists[p * cap + n] = ((s + base) << 7) | ((code & 15) << 3) | outs[s]
            counts[p] = n + live[s]
            return carry

        lax.fori_loop(0, ks.shape[0], step, 0)

    scan(own_k, own_out, own_live, 0)
    scan(help_k, help_out, help_live, n_own)
    for p in range(PIECES):
        for w in range(SCAN):
            lists[p * cap + counts[p] + w] = OB
    fetch_own.wait()
    fetch_help.wait()


def pack_kernel(*refs):
    groups, (head, tail) = refs[:NZL], refs[NZL:NZL + 2]
    gone_v, gone_s, sem = refs[NZL + 2:]
    lane = lax.broadcasted_iota(jnp.int32, (8, TILE), 1)
    gone = jnp.zeros((8, TILE), jnp.int32)
    for slot in range(LINE):
        row = groups[slot // NZH][slot % NZH, pl.ds(0, 16), :].astype(jnp.float32)[:1]
        gone = jnp.where((lane == slot) & (row == jnp.inf), 1, gone)
    gone_v[...] = gone
    copy = pltpu.make_async_copy(gone_v, gone_s, sem.at[0])
    copy.start()
    copy.wait()
    lane = lax.broadcasted_iota(jnp.int32, (META, TILE), 1)
    places = jnp.full((META, TILE), ABSENT, jnp.int32)
    n = jnp.int32(0)
    for slot in range(LINE):
        here = gone_s[0, slot] == 0
        tile = groups[slot // NZH].at[slot % NZH]

        @pl.when(here & (n < PACK))
        def _():
            head[pl.ds(pl.multiple_of(n * TILE, TILE), TILE), :] = tile[...]

        @pl.when(here & (n >= PACK))
        def _():
            tail[pl.ds(pl.multiple_of((n - PACK) * TILE, TILE), TILE), :] = tile[...]

        places = jnp.where(lane == slot, jnp.where(here, n, ABSENT), places)
        n = n + jnp.where(here, 1, 0)
    late = (places >= PACK) & (places < ABSENT)
    first = jnp.where(late, LATER, places)
    first = jnp.where(lane == LINE, jnp.where(n > PACK, 1, 0), first)
    second = jnp.where(late, places - PACK, ABSENT)
    second = jnp.where(lane == LINE, 0, second)
    head[pl.ds(PACK * TILE, META), :] = first.astype(jnp.float32).astype(head.dtype)
    tail[pl.ds(REST * TILE, META), :] = second.astype(jnp.float32).astype(tail.dtype)


def pack(groups):
    vmem = pl.BlockSpec(memory_space=pltpu.VMEM)
    return pl.pallas_call(
        pack_kernel,
        out_shape=(
            jax.ShapeDtypeStruct((PACK * TILE + META, TILE), jnp.bfloat16),
            jax.ShapeDtypeStruct((REST * TILE + META, TILE), jnp.bfloat16),
        ),
        in_specs=[vmem] * len(groups),
        out_specs=(vmem, vmem),
        scratch_shapes=[
            pltpu.VMEM((8, TILE), jnp.int32),
            pltpu.SMEM((8, TILE), jnp.int32),
            pltpu.SemaphoreType.DMA((1,)),
        ],
        name="pack",
        compiler_params=pltpu.CompilerParams(vmem_limit_bytes=24 << 20),
    )(*groups)


def task_kernel(ids, places, last, lists, counts, tiles, acc_in, over_in, *rest):
    pieces, rest = rest[:len(ids)], rest[len(ids):]
    outs, (acc, meta_v, meta_s, picked, sem) = rest[:-5], rest[-5:]
    cap = lists.shape[0] // PIECES
    for j, piece in enumerate(pieces):
        meta = piece[pl.ds(places * TILE, META), :].astype(jnp.float32).astype(jnp.int32)
        meta_v[pl.ds(j, 1), :] = meta[:1]
    copy = pltpu.make_async_copy(meta_v, meta_s, sem.at[0])
    copy.start()
    acc[pl.ds(0, OB)] = acc_in[...]
    copy.wait()
    over = over_in[0]
    for j, (p, amps) in enumerate(zip(ids, pieces)):
        over = over + meta_s[j, LINE]

        count = counts[p]

        def pick(g, n, p=p, j=j, count=count):
            for u in range(SCAN):
                e = g * SCAN + u
                entry = lists[p * cap + e]
                place = meta_s[j, (entry >> 3) & 15]
                picked[n] = (entry & ~127) | (place << 3) | (entry & 7)
                n = n + jnp.where((place < places) & (e < count), 1, 0)
            return n

        n = lax.fori_loop(0, (count + SCAN - 1) >> 3, pick, 0)
        for w in range(WIDE):
            picked[n + w] = OB

        def step(g, carry, amps=amps):
            outputs, prods = [], []
            for w in range(WIDE):
                entry = picked[g * WIDE + w]
                outputs.append(entry & 7)
                place = (entry >> 3) & 15
                a = amps[pl.ds(pl.multiple_of(place * TILE, TILE), TILE), :]
                b = tiles[entry >> 7]
                prods.append(jnp.dot(a, b, preferred_element_type=jnp.float32))
            for w in range(WIDE):
                acc[outputs[w]] += prods[w]
            return carry

        lax.fori_loop(0, (n + WIDE - 1) >> 2, step, 0)
    if last:
        for o in range(OB):
            outs[2][:, o * TILE:(o + 1) * TILE] = acc[o].astype(outs[2].dtype)
    outs[0][...] = acc[pl.ds(0, OB)]
    outs[1][0] = over


def run_tasks(ids, pieces, acc_in, last, lists, counts, tiles, places=PACK):
    smem = pl.BlockSpec(memory_space=pltpu.SMEM)
    vmem = pl.BlockSpec(memory_space=pltpu.VMEM)
    out_shape = [jax.ShapeDtypeStruct((OB, TILE, TILE), jnp.float32), jax.ShapeDtypeStruct((1,), jnp.int32)]
    out_specs = [vmem, smem]
    if last:
        out_shape.append(jax.ShapeDtypeStruct((TILE, OB * TILE), jnp.bfloat16))
        out_specs.append(vmem)
    n = tiles.shape[0] * len(ids) // PIECES
    return pl.pallas_call(
        functools.partial(task_kernel, ids, places, last),
        out_shape=out_shape,
        in_specs=[smem, smem, vmem, vmem, smem] + [vmem] * len(pieces),
        out_specs=out_specs,
        scratch_shapes=[
            pltpu.VMEM((OB + 1, TILE, TILE), jnp.float32),
            pltpu.VMEM((8, TILE), jnp.int32),
            pltpu.SMEM((8, TILE), jnp.int32),
            pltpu.SMEM((tiles.shape[0] + 8,), jnp.int32),
            pltpu.SemaphoreType.DMA((1,)),
        ],
        compiler_params=pltpu.CompilerParams(vmem_limit_bytes=24 << 20),
        cost_estimate=pl.CostEstimate(flops=n * TILE ** 3, bytes_accessed=n * TILE, transcendentals=0),
        name="tasks" + "".join(str(p) for p in ids),
    )(lists, counts, tiles, *acc_in, *pieces)


def prepare(own_tiles, own_k, own_out, own_live, help_tiles, help_k, help_out, help_live):
    me, k = lax.axis_index("col"), jnp.arange(COLS, dtype=jnp.int32)
    c, y = (me ^ k) & 1, (me ^ k) >> 5
    zl, zh = ((me >> 1) - (k >> 1)) & 3, ((me >> 3) - (k >> 3)) & 3
    table = ((c * NY + y) * NZL + zl) * NZH + zh
    n = own_k.shape[0] + help_k.shape[0]
    smem = pl.BlockSpec(memory_space=pltpu.SMEM)
    hbm = pl.BlockSpec(memory_space=pltpu.HBM)
    scalars = (own_k, own_out, own_live, help_k, help_out, help_live, table)
    return pl.pallas_call(
        prep_kernel,
        out_shape=(
            jax.ShapeDtypeStruct((PIECES * (n + 8),), jnp.int32),
            jax.ShapeDtypeStruct((PIECES,), jnp.int32),
            pltpu.VMEM((n, TILE, TILE), jnp.bfloat16),
        ),
        in_specs=[hbm] * 9,
        out_specs=(smem, smem, pl.BlockSpec(memory_space=pltpu.VMEM)),
        scratch_shapes=[pltpu.SemaphoreType.DMA((2 + len(scalars),))]
        + [pltpu.SMEM(v.shape, jnp.int32) for v in scalars],
        name="prep",
        compiler_params=pltpu.CompilerParams(vmem_limit_bytes=24 << 20),
        cost_estimate=pl.CostEstimate(flops=0, bytes_accessed=8 << 20, transcendentals=0),
    )(*[pltpu.with_memory_space_constraint(v, pltpu.HBM) for v in (*scalars, own_tiles, help_tiles)])


def shards(
    amplitudes,
    amp_kept,
    own_tiles,
    own_k,
    own_out,
    own_live,
    help_tiles,
    help_k,
    help_out,
    help_live,
):
    kept = jnp.where(amp_kept != 0, amplitudes * amp_kept.astype(jnp.bfloat16), jnp.inf).astype(jnp.bfloat16)
    first = jnp.stack([kept] + [move(kept, zh=k) for k in (1, 2, 3)])
    head, tail = pack([first] + [move(first, zl=k) for k in (1, 2, 3)])
    lists, counts, tiles = prepare(
        own_tiles, own_k, own_out, own_live, help_tiles, help_k, help_out, help_live)
    ys = {k: move(head, y=k) for k in (1, 3, 2)}
    tasks = functools.partial(run_tasks, lists=lists, counts=counts, tiles=tiles)
    acc = (jnp.zeros((OB, TILE, TILE), jnp.float32), jnp.zeros((1,), jnp.int32))
    acc = tasks((0, NY), [head, move(head, c=1)], acc, False)
    ys[1], acc = lax.optimization_barrier((ys[1], acc))
    ys_c = {k: move(ys[k], c=1) for k in (1, 3, 2)}
    acc = tasks((1, 3, 2), [ys[1], ys[3], ys[2]], acc, False)
    total, over, out = tasks((NY + 1, NY + 3, NY + 2), [ys_c[1], ys_c[3], ys_c[2]], acc, True)

    def second_round(tail, total, over, out):
        line = [tail] + [move(tail, y=k) for k in (1, 2, 3)]
        pieces = line + [move(v, c=1) for v in line]
        return tasks(tuple(range(PIECES)), pieces, (total, over), True, places=REST)[2]

    return lax.cond(over[0] > 0, second_round, lambda tail, total, over, out: out, tail, total, over, out)


def solution(mesh):
    return jax.shard_map(
        shards,
        mesh=mesh,
        in_specs=(
            P("row", "col"),
            P("row", "col"),
            P("col", None, None),
            P("col"),
            P("col"),
            P("col"),
            P("col", None, None),
            P("col"),
            P("col"),
            P("col"),
        ),
        out_specs=P("row", "col"),
        check_vma=False,
    )
```

```python
import functools

import jax
import jax.numpy as jnp
import numpy as np
from jax import lax
from jax.experimental import pallas as pl
from jax.experimental.pallas import tpu as pltpu
from jax.sharding import PartitionSpec as P

TILE = 128
OB = 4
NY, NZH, NZL, NC = 4, 4, 4, 2
COLS = NY * NZH * NZL * NC
LINE = NZH * NZL
PHASES = 3
WIDE = 8
SCAN = 8
PACK = 10
REST = LINE - PACK
META = 16
ROWS = PACK * 128 + META
ORDER = (2, 1, 3)
ABSENT, LATER = 99, 50


def move(x, y=0, zh=0, zl=0, c=0):
    pairs = []
    for i in range(COLS):
        far, near = (i // (NC * NZL) + zh) % NZH, (i // NC + zl) % NZL
        here = ((i // (NC * LINE) ^ y) * NZH + far) * NZL + near
        pairs.append((i, here * NC + (i % NC ^ c)))
    return lax.ppermute(x, "col", pairs)


def prep_kernel(own_k, own_out, own_live, help_k, help_out, help_live, table, own_tiles, help_tiles,
                lists, counts, tiles, sems, *held):
    n_own, n_help = own_k.shape[0], help_k.shape[0]
    cap = lists.shape[0] // PHASES
    loads = []
    for j, ref in enumerate((own_k, own_out, own_live, help_k, help_out, help_live, table)):
        loads.append(pltpu.make_async_copy(ref, held[j], sems.at[2 + j]))
        loads[j].start()
    own_k, own_out, own_live, help_k, help_out, help_live, table = held
    fetch_own = pltpu.make_async_copy(own_tiles, tiles.at[pl.ds(0, n_own)], sems.at[0])
    fetch_help = pltpu.make_async_copy(help_tiles, tiles.at[pl.ds(n_own, n_help)], sems.at[1])
    fetch_own.start()
    fetch_help.start()
    for p in range(PHASES):
        counts[p] = 0
    for load in loads:
        load.wait()

    def scan(ks, outs, live, base):
        def step(s, carry):
            code = table[ks[s]]
            p = code >> 6
            n = counts[p]
            lists[p * cap + n] = ((s + base) << 9) | ((code & 63) << 3) | outs[s]
            counts[p] = n + live[s]
            return carry

        lax.fori_loop(0, ks.shape[0], step, 0)

    scan(own_k, own_out, own_live, 0)
    scan(help_k, help_out, help_live, n_own)
    for p in range(PHASES):
        for w in range(SCAN):
            lists[p * cap + counts[p] + w] = OB
    fetch_own.wait()
    fetch_help.wait()


def pack_kernel(*refs):
    groups, (head, tail) = refs[:NZL], refs[NZL:NZL + 2]
    gone_v, gone_s, sem = refs[NZL + 2:]
    lane = lax.broadcasted_iota(jnp.int32, (8, TILE), 1)
    gone = jnp.zeros((8, TILE), jnp.int32)
    for slot in range(LINE):
        row = groups[slot // NZH][slot % NZH, pl.ds(0, 16), :].astype(jnp.float32)[:1]
        gone = jnp.where((lane == slot) & (row == jnp.inf), 1, gone)
    gone_v[...] = gone
    copy = pltpu.make_async_copy(gone_v, gone_s, sem.at[0])
    copy.start()
    copy.wait()
    lane = lax.broadcasted_iota(jnp.int32, (META, TILE), 1)
    places = jnp.full((META, TILE), ABSENT, jnp.int32)
    n = jnp.int32(0)
    for slot in range(LINE):
        here = gone_s[0, slot] == 0
        tile = groups[slot // NZH].at[slot % NZH]

        @pl.when(here & (n < PACK))
        def _():
            head[pl.ds(pl.multiple_of(n * TILE, TILE), TILE), :] = tile[...]

        @pl.when(here & (n >= PACK))
        def _():
            tail[pl.ds(pl.multiple_of((n - PACK) * TILE, TILE), TILE), :] = tile[...]

        places = jnp.where(lane == slot, jnp.where(here, n, ABSENT), places)
        n = n + jnp.where(here, 1, 0)
    late = (places >= PACK) & (places < ABSENT)
    first = jnp.where(late, LATER, places)
    first = jnp.where(lane == LINE, jnp.where(n > PACK, 1, 0), first)
    second = jnp.where(late, places - PACK, ABSENT)
    second = jnp.where(lane == LINE, 0, second)
    head[pl.ds(PACK * TILE, META), :] = first.astype(jnp.float32).astype(head.dtype)
    tail[pl.ds(REST * TILE, META), :] = second.astype(jnp.float32).astype(tail.dtype)


def pack(groups):
    vmem = pl.BlockSpec(memory_space=pltpu.VMEM)
    return pl.pallas_call(
        pack_kernel,
        out_shape=(
            jax.ShapeDtypeStruct((PACK * TILE + META, TILE), jnp.bfloat16),
            jax.ShapeDtypeStruct((REST * TILE + META, TILE), jnp.bfloat16),
        ),
        in_specs=[vmem] * len(groups),
        out_specs=(vmem, vmem),
        scratch_shapes=[
            pltpu.VMEM((8, TILE), jnp.int32),
            pltpu.SMEM((8, TILE), jnp.int32),
            pltpu.SemaphoreType.DMA((1,)),
        ],
        name="pack",
        compiler_params=pltpu.CompilerParams(vmem_limit_bytes=24 << 20),
    )(*groups)


def task_kernel(phase, places, last, lists, counts, tiles, acc_in, over_in, *rest):
    outs, (acc, amps, meta_v, meta_s, picked, sem) = rest[:-6], rest[-6:]
    n_pieces = len(outs) - (3 if last else 2)
    pieces, outs = outs[:n_pieces], outs[n_pieces:]
    cap = lists.shape[0] // PHASES
    for j, piece in enumerate(pieces):
        meta = piece[pl.ds(places * TILE, META), :].astype(jnp.float32).astype(jnp.int32)
        meta_v[pl.ds(j, 1), :] = meta[:1]
    copy = pltpu.make_async_copy(meta_v, meta_s, sem.at[n_pieces])
    copy.start()
    gathers = []
    for j, piece in enumerate(pieces):
        gathers.append(pltpu.make_async_copy(piece, amps.at[pl.ds(j * ROWS, piece.shape[0])], sem.at[j]))
        gathers[j].start()
    acc[pl.ds(0, OB)] = acc_in[...]
    copy.wait()
    over = over_in[0]
    for j in range(n_pieces):
        over = over + meta_s[j, LINE]
    count = counts[phase]

    def pick(g, n):
        for u in range(SCAN):
            e = g * SCAN + u
            entry = lists[phase * cap + e]
            place = meta_s[(entry >> 7) & 3, (entry >> 3) & 15]
            picked[n] = (entry & ~120) | ((place & 15) << 3)
            n = n + jnp.where((place < places) & (e < count), 1, 0)
        return n

    n = lax.fori_loop(0, (count + SCAN - 1) >> 3, pick, 0)
    for w in range(WIDE):
        picked[n + w] = OB
    for gather in gathers:
        gather.wait()

    def step(g, carry):
        outputs, prods = [], []
        for w in range(WIDE):
            entry = picked[g * WIDE + w]
            outputs.append(entry & 7)
            row = ((entry >> 7) & 3) * ROWS + ((entry >> 3) & 15) * TILE
            a = amps[pl.ds(pl.multiple_of(row, 16), TILE), :]
            b = tiles[entry >> 9]
            prods.append(jnp.dot(a, b, preferred_element_type=jnp.float32))
        for w in range(WIDE):
            acc[outputs[w]] += prods[w]
        return carry

    lax.fori_loop(0, (n + WIDE - 1) >> 3, step, 0)
    if last:
        for o in range(OB):
            outs[2][:, o * TILE:(o + 1) * TILE] = acc[o].astype(outs[2].dtype)
    outs[0][...] = acc[pl.ds(0, OB)]
    outs[1][0] = over


def run_tasks(phase, pieces, acc_in, last, lists, counts, tiles, places=PACK):
    smem = pl.BlockSpec(memory_space=pltpu.SMEM)
    vmem = pl.BlockSpec(memory_space=pltpu.VMEM)
    out_shape = [jax.ShapeDtypeStruct((OB, TILE, TILE), jnp.float32), jax.ShapeDtypeStruct((1,), jnp.int32)]
    out_specs = [vmem, smem]
    if last:
        out_shape.append(jax.ShapeDtypeStruct((TILE, OB * TILE), jnp.bfloat16))
        out_specs.append(vmem)
    n = tiles.shape[0] * len(pieces) // (NC * NY)
    return pl.pallas_call(
        functools.partial(task_kernel, phase, places, last),
        out_shape=out_shape,
        in_specs=[smem, smem, vmem, vmem, smem] + [vmem] * len(pieces),
        out_specs=out_specs,
        scratch_shapes=[
            pltpu.VMEM((OB + 1, TILE, TILE), jnp.float32),
            pltpu.VMEM((len(pieces) * ROWS, TILE), jnp.bfloat16),
            pltpu.VMEM((8, TILE), jnp.int32),
            pltpu.SMEM((8, TILE), jnp.int32),
            pltpu.SMEM((tiles.shape[0] + 16,), jnp.int32),
            pltpu.SemaphoreType.DMA((len(pieces) + 1,)),
        ],
        compiler_params=pltpu.CompilerParams(vmem_limit_bytes=24 << 20),
        cost_estimate=pl.CostEstimate(flops=n * 20 * TILE ** 3, bytes_accessed=8 << 20, transcendentals=0),
        name=f"tasks{phase}",
    )(lists, counts, tiles, *acc_in, *pieces)


def prepare(own_tiles, own_k, own_out, own_live, help_tiles, help_k, help_out, help_live):
    me, k = lax.axis_index("col"), jnp.arange(COLS, dtype=jnp.int32)
    c, y = (me ^ k) & 1, (me ^ k) >> 5
    zl, zh = ((me >> 1) - (k >> 1)) & 3, ((me >> 3) - (k >> 3)) & 3
    rank = sum(jnp.where(y == k, j, 0) for j, k in enumerate(ORDER))
    group = jnp.where(y == 0, c, (1 + c) * 4 + rank)
    table = (group * NZL + zl) * NZH + zh
    n = own_k.shape[0] + help_k.shape[0]
    smem = pl.BlockSpec(memory_space=pltpu.SMEM)
    hbm = pl.BlockSpec(memory_space=pltpu.HBM)
    scalars = (own_k, own_out, own_live, help_k, help_out, help_live, table)
    return pl.pallas_call(
        prep_kernel,
        out_shape=(
            jax.ShapeDtypeStruct((PHASES * (n + 8),), jnp.int32),
            jax.ShapeDtypeStruct((PHASES,), jnp.int32),
            pltpu.VMEM((n, TILE, TILE), jnp.bfloat16),
        ),
        in_specs=[hbm] * 9,
        out_specs=(smem, smem, pl.BlockSpec(memory_space=pltpu.VMEM)),
        scratch_shapes=[pltpu.SemaphoreType.DMA((2 + len(scalars),))]
        + [pltpu.SMEM(v.shape, jnp.int32) for v in scalars],
        name="prep",
        compiler_params=pltpu.CompilerParams(vmem_limit_bytes=24 << 20),
        cost_estimate=pl.CostEstimate(flops=0, bytes_accessed=8 << 20, transcendentals=0),
    )(*[pltpu.with_memory_space_constraint(v, pltpu.HBM) for v in (*scalars, own_tiles, help_tiles)])


def shards(
    amplitudes,
    amp_kept,
    own_tiles,
    own_k,
    own_out,
    own_live,
    help_tiles,
    help_k,
    help_out,
    help_live,
):
    kept = jnp.where(amp_kept != 0, amplitudes * amp_kept.astype(jnp.bfloat16), jnp.inf).astype(jnp.bfloat16)
    first = jnp.stack([kept] + [move(kept, zh=k) for k in (1, 2, 3)])
    head, tail = pack([first] + [move(first, zl=k) for k in (1, 2, 3)])
    lists, counts, tiles = prepare(
        own_tiles, own_k, own_out, own_live, help_tiles, help_k, help_out, help_live)
    tasks = functools.partial(run_tasks, lists=lists, counts=counts, tiles=tiles)
    ys = [move(head, y=k) for k in ORDER]
    acc = (jnp.zeros((OB, TILE, TILE), jnp.float32), jnp.zeros((1,), jnp.int32))
    acc = tasks(0, [head, move(head, c=1)], acc, False)
    ys[0], acc = lax.optimization_barrier((ys[0], acc))
    ys_c = [move(v, c=1) for v in ys]
    acc = tasks(1, ys, acc, False)
    total, over, out = tasks(2, ys_c, acc, True)

    def second_round(tail, total, over, out):
        ys = [move(tail, y=k) for k in ORDER]
        acc = tasks(0, [tail, move(tail, c=1)], (total, over), False, places=REST)
        acc = tasks(1, ys, acc, False, places=REST)
        return tasks(2, [move(v, c=1) for v in ys], acc, True, places=REST)[2]

    return lax.cond(over[0] > 0, second_round, lambda tail, total, over, out: out, tail, total, over, out)


def solution(mesh):
    return jax.shard_map(
        shards,
        mesh=mesh,
        in_specs=(
            P("row", "col"),
            P("row", "col"),
            P("col", None, None),
            P("col"),
            P("col"),
            P("col"),
            P("col", None, None),
            P("col"),
            P("col"),
            P("col"),
        ),
        out_specs=P("row", "col"),
        check_vma=False,
    )
```

```python
import functools

import jax
import jax.numpy as jnp
import numpy as np
from jax import lax
from jax.experimental import pallas as pl
from jax.experimental.pallas import tpu as pltpu
from jax.sharding import PartitionSpec as P

TILE = 128
OB = 4
NY, NZH, NZL, NC = 4, 4, 4, 2
COLS = NY * NZH * NZL * NC
LINE = NZH * NZL
PHASES = 3
WIDE = 8
SCAN = 8
PACK = 10
REST = LINE - PACK
META = 16
ORDER = (2, 1, 3)
ABSENT, LATER = 99, 50


def move(x, y=0, zh=0, zl=0, c=0):
    pairs = []
    for i in range(COLS):
        far, near = (i // (NC * NZL) + zh) % NZH, (i // NC + zl) % NZL
        here = ((i // (NC * LINE) ^ y) * NZH + far) * NZL + near
        pairs.append((i, here * NC + (i % NC ^ c)))
    return lax.ppermute(x, "col", pairs)


def prep_kernel(own_k, own_out, own_live, help_k, help_out, help_live, table, own_tiles, help_tiles,
                lists, tiles, sems, *held):
    n_own, n_help = own_k.shape[0], help_k.shape[0]
    cap = n_own + n_help + SCAN
    loads = []
    for j, ref in enumerate((own_k, own_out, own_live, help_k, help_out, help_live, table)):
        loads.append(pltpu.make_async_copy(ref, held[j], sems.at[2 + j]))
        loads[j].start()
    own_k, own_out, own_live, help_k, help_out, help_live, table = held
    fetch_own = pltpu.make_async_copy(own_tiles, tiles.at[pl.ds(0, n_own)], sems.at[0])
    fetch_help = pltpu.make_async_copy(help_tiles, tiles.at[pl.ds(n_own, n_help)], sems.at[1])
    fetch_own.start()
    fetch_help.start()
    for p in range(PHASES):
        lists[PHASES * cap + p] = 0
    for load in loads:
        load.wait()

    def scan(ks, outs, live, base):
        def step(s, carry):
            code = table[ks[s]]
            p = code >> 6
            n = lists[PHASES * cap + p]
            lists[p * cap + n] = ((s + base) << 9) | ((code & 63) << 3) | outs[s]
            lists[PHASES * cap + p] = n + live[s]
            return carry

        lax.fori_loop(0, ks.shape[0], step, 0)

    scan(own_k, own_out, own_live, 0)
    scan(help_k, help_out, help_live, n_own)
    for p in range(PHASES):
        n = lists[PHASES * cap + p]
        for w in range(SCAN):
            lists[p * cap + n + w] = OB
    fetch_own.wait()
    fetch_help.wait()


def pack_kernel(*refs):
    groups, (head, tail) = refs[:NZL], refs[NZL:NZL + 2]
    gone_v, gone_s, sem = refs[NZL + 2:]
    lane = lax.broadcasted_iota(jnp.int32, (8, TILE), 1)
    gone = jnp.zeros((8, TILE), jnp.int32)
    for slot in range(LINE):
        row = groups[slot // NZH][slot % NZH, pl.ds(0, 16), :].astype(jnp.float32)[:1]
        gone = jnp.where((lane == slot) & (row == jnp.inf), 1, gone)
    gone_v[...] = gone
    copy = pltpu.make_async_copy(gone_v, gone_s, sem.at[0])
    copy.start()
    copy.wait()
    lane = lax.broadcasted_iota(jnp.int32, (META, TILE), 1)
    places = jnp.full((META, TILE), ABSENT, jnp.int32)
    n = jnp.int32(0)
    for slot in range(LINE):
        here = gone_s[0, slot] == 0
        tile = groups[slot // NZH].at[slot % NZH]

        @pl.when(here & (n < PACK))
        def _():
            head[pl.ds(pl.multiple_of(n * TILE, TILE), TILE), :] = tile[...]

        @pl.when(here & (n >= PACK))
        def _():
            tail[pl.ds(pl.multiple_of((n - PACK) * TILE, TILE), TILE), :] = tile[...]

        places = jnp.where(lane == slot, jnp.where(here, n, ABSENT), places)
        n = n + jnp.where(here, 1, 0)
    late = (places >= PACK) & (places < ABSENT)
    first = jnp.where(late, LATER, places)
    first = jnp.where(lane == LINE, jnp.where(n > PACK, 1, 0), first)
    second = jnp.where(late, places - PACK, ABSENT)
    second = jnp.where(lane == LINE, 0, second)
    head[pl.ds(PACK * TILE, META), :] = first.astype(jnp.float32).astype(head.dtype)
    tail[pl.ds(REST * TILE, META), :] = second.astype(jnp.float32).astype(tail.dtype)


def pack(groups):
    vmem = pl.BlockSpec(memory_space=pltpu.VMEM)
    return pl.pallas_call(
        pack_kernel,
        out_shape=(
            jax.ShapeDtypeStruct((PACK * TILE + META, TILE), jnp.bfloat16),
            jax.ShapeDtypeStruct((REST * TILE + META, TILE), jnp.bfloat16),
        ),
        in_specs=[vmem] * len(groups),
        out_specs=(vmem, vmem),
        scratch_shapes=[
            pltpu.VMEM((8, TILE), jnp.int32),
            pltpu.SMEM((8, TILE), jnp.int32),
            pltpu.SemaphoreType.DMA((1,)),
        ],
        name="pack",
        compiler_params=pltpu.CompilerParams(vmem_limit_bytes=24 << 20),
    )(*groups)


def task_kernel(phase, places, last, lists_v, tiles, acc_in, over_in, *rest):
    outs, (acc, meta_v, meta_s, lists, picked, sem) = rest[:-6], rest[-6:]
    n_pieces = len(outs) - (3 if last else 2)
    pieces, outs = outs[:n_pieces], outs[n_pieces:]
    cap = tiles.shape[0] + SCAN
    load = pltpu.make_async_copy(lists_v, lists, sem.at[0])
    load.start()
    over = over_in[...]
    for j, piece in enumerate(pieces):
        meta = piece[pl.ds(places * TILE, META), :].astype(jnp.float32).astype(jnp.int32)
        meta_v[pl.ds(j, 1), :] = meta[:1]
        over = over + meta[:8]
    meta_v[pl.ds(n_pieces, 1), :] = over[:1]
    copy = pltpu.make_async_copy(meta_v, meta_s, sem.at[1])
    copy.start()
    acc[pl.ds(0, OB)] = acc_in[...]
    load.wait()
    copy.wait()
    count = lists[PHASES * cap + phase]

    def pick(g, n):
        for u in range(SCAN):
            e = g * SCAN + u
            entry = lists[phase * cap + e]
            place = meta_s[(entry >> 7) & 3, (entry >> 3) & 15]
            picked[n] = (entry & ~120) | ((place & 15) << 3)
            n = n + jnp.where((place < places) & (e < count), 1, 0)
        return n

    n = lax.fori_loop(0, (count + SCAN - 1) >> 3, pick, 0)
    for w in range(WIDE):
        picked[n + w] = OB

    def step(g, carry):
        outputs, prods = [], []
        for w in range(WIDE):
            entry = picked[g * WIDE + w]
            outputs.append(entry & 7)
            rows = pl.ds(pl.multiple_of(((entry >> 3) & 15) * TILE, TILE), TILE)
            a = pieces[0][rows, :]
            for j in range(1, n_pieces):
                a = jnp.where(((entry >> 7) & 3) == j, pieces[j][rows, :], a)
            b = tiles[entry >> 9]
            prods.append(jnp.dot(a, b, preferred_element_type=jnp.float32))
        for w in range(WIDE):
            acc[outputs[w]] += prods[w]
        return carry

    lax.fori_loop(0, (n + WIDE - 1) >> 3, step, 0)
    if last:
        for o in range(OB):
            outs[2][:, o * TILE:(o + 1) * TILE] = acc[o].astype(outs[2].dtype)
    outs[0][...] = acc[pl.ds(0, OB)]
    if last:
        outs[1][0] = meta_s[n_pieces, LINE]
    else:
        outs[1][...] = over


def run_tasks(phase, pieces, acc_in, last, lists, tiles, places=PACK):
    smem = pl.BlockSpec(memory_space=pltpu.SMEM)
    vmem = pl.BlockSpec(memory_space=pltpu.VMEM)
    out_shape = [jax.ShapeDtypeStruct((OB, TILE, TILE), jnp.float32), jax.ShapeDtypeStruct((1,) if last else (8, TILE), jnp.int32)]
    out_specs = [vmem, smem if last else vmem]
    if last:
        out_shape.append(jax.ShapeDtypeStruct((TILE, OB * TILE), jnp.bfloat16))
        out_specs.append(vmem)
    n = tiles.shape[0] * len(pieces) // (NC * NY)
    return pl.pallas_call(
        functools.partial(task_kernel, phase, places, last),
        out_shape=out_shape,
        in_specs=[vmem] * (4 + len(pieces)),
        out_specs=out_specs,
        scratch_shapes=[
            pltpu.VMEM((OB + 1, TILE, TILE), jnp.float32),
            pltpu.VMEM((8, TILE), jnp.int32),
            pltpu.SMEM((8, TILE), jnp.int32),
            pltpu.SMEM(lists.shape, jnp.int32),
            pltpu.SMEM((tiles.shape[0] + 16,), jnp.int32),
            pltpu.SemaphoreType.DMA((2,)),
        ],
        compiler_params=pltpu.CompilerParams(vmem_limit_bytes=24 << 20),
        cost_estimate=pl.CostEstimate(flops=n * 20 * TILE ** 3, bytes_accessed=8 << 20, transcendentals=0),
        name=f"tasks{phase}",
    )(lists, tiles, *acc_in, *pieces)


def prepare(own_tiles, own_k, own_out, own_live, help_tiles, help_k, help_out, help_live):
    me, k = lax.axis_index("col"), jnp.arange(COLS, dtype=jnp.int32)
    c, y = (me ^ k) & 1, (me ^ k) >> 5
    zl, zh = ((me >> 1) - (k >> 1)) & 3, ((me >> 3) - (k >> 3)) & 3
    rank = sum(jnp.where(y == k, j, 0) for j, k in enumerate(ORDER))
    group = jnp.where(y == 0, c, (1 + c) * 4 + rank)
    table = (group * NZL + zl) * NZH + zh
    n = own_k.shape[0] + help_k.shape[0]
    smem = pl.BlockSpec(memory_space=pltpu.SMEM)
    hbm = pl.BlockSpec(memory_space=pltpu.HBM)
    scalars = (own_k, own_out, own_live, help_k, help_out, help_live, table)
    return pl.pallas_call(
        prep_kernel,
        out_shape=(
            jax.ShapeDtypeStruct((PHASES * (n + SCAN) + SCAN,), jnp.int32),
            pltpu.VMEM((n, TILE, TILE), jnp.bfloat16),
        ),
        in_specs=[hbm] * 9,
        out_specs=(smem, pl.BlockSpec(memory_space=pltpu.VMEM)),
        scratch_shapes=[pltpu.SemaphoreType.DMA((2 + len(scalars),))]
        + [pltpu.SMEM(v.shape, jnp.int32) for v in scalars],
        name="prep",
        compiler_params=pltpu.CompilerParams(vmem_limit_bytes=24 << 20),
        cost_estimate=pl.CostEstimate(flops=0, bytes_accessed=8 << 20, transcendentals=0),
    )(*[pltpu.with_memory_space_constraint(v, pltpu.HBM) for v in (*scalars, own_tiles, help_tiles)])


def shards(
    amplitudes,
    amp_kept,
    own_tiles,
    own_k,
    own_out,
    own_live,
    help_tiles,
    help_k,
    help_out,
    help_live,
):
    kept = jnp.where(amp_kept != 0, amplitudes * amp_kept.astype(jnp.bfloat16), jnp.inf).astype(jnp.bfloat16)
    first = jnp.stack([kept] + [move(kept, zh=k) for k in (1, 2, 3)])
    head, tail = pack([first] + [move(first, zl=k) for k in (1, 2, 3)])
    lists, tiles = prepare(
        own_tiles, own_k, own_out, own_live, help_tiles, help_k, help_out, help_live)
    ys = [move(head, y=k) for k in ORDER]
    own_head, lists = lax.optimization_barrier((head, lists))
    tasks = functools.partial(run_tasks, lists=lists, tiles=tiles)
    acc = (jnp.zeros((OB, TILE, TILE), jnp.float32), jnp.zeros((8, TILE), jnp.int32))
    acc = tasks(0, [head, move(own_head, c=1)], acc, False)
    ys[0], acc = lax.optimization_barrier((ys[0], acc))
    ys_c = [move(v, c=1) for v in ys]
    acc_own = tasks(1, ys, acc, False)
    total, over, out = tasks(2, ys_c, acc_own, True)

    def second_round(tail, total, out):
        ys = [move(tail, y=k) for k in ORDER]
        acc = (total, jnp.zeros((8, TILE), jnp.int32))
        acc = tasks(0, [tail, move(tail, c=1)], acc, False, places=REST)
        acc = tasks(1, ys, acc, False, places=REST)
        return tasks(2, [move(v, c=1) for v in ys], acc, True, places=REST)[2]

    return lax.cond(over[0] > 0, second_round, lambda tail, total, out: out, tail, total, out)


def solution(mesh):
    return jax.shard_map(
        shards,
        mesh=mesh,
        in_specs=(
            P("row", "col"),
            P("row", "col"),
            P("col", None, None),
            P("col"),
            P("col"),
            P("col"),
            P("col", None, None),
            P("col"),
            P("col"),
            P("col"),
        ),
        out_specs=P("row", "col"),
        check_vma=False,
    )
```

```python
import functools

import jax
import jax.numpy as jnp
import numpy as np
from jax import lax
from jax.experimental import pallas as pl
from jax.experimental.pallas import tpu as pltpu
from jax.sharding import PartitionSpec as P

TILE = 128
OB = 4
NY, NZH, NZL, NC = 4, 4, 4, 2
COLS = NY * NZH * NZL * NC
LINE = NZH * NZL
PHASES = 3
WIDE = 8
SCAN = 8
PACK = 10
REST = LINE - PACK
META = 16
PLAN = (((0, 0), (0, 1), (2, 0)), ((1, 0), (3, 0), (2, 1)), ((1, 1), (3, 1)))
ABSENT, LATER = 99, 50


def move(x, y=0, zh=0, zl=0, c=0):
    pairs = []
    for i in range(COLS):
        far, near = (i // (NC * NZL) + zh) % NZH, (i // NC + zl) % NZL
        here = ((i // (NC * LINE) ^ y) * NZH + far) * NZL + near
        pairs.append((i, here * NC + (i % NC ^ c)))
    return lax.ppermute(x, "col", pairs)


def prep_kernel(own_k, own_out, own_live, help_k, help_out, help_live, table, own_tiles, help_tiles,
                lists, tiles, sems, *held):
    n_own, n_help = own_k.shape[0], help_k.shape[0]
    cap = n_own + n_help + SCAN
    loads = []
    for j, ref in enumerate((own_k, own_out, own_live, help_k, help_out, help_live, table)):
        loads.append(pltpu.make_async_copy(ref, held[j], sems.at[2 + j]))
        loads[j].start()
    own_k, own_out, own_live, help_k, help_out, help_live, table = held
    fetch_own = pltpu.make_async_copy(own_tiles, tiles.at[pl.ds(0, n_own)], sems.at[0])
    fetch_help = pltpu.make_async_copy(help_tiles, tiles.at[pl.ds(n_own, n_help)], sems.at[1])
    fetch_own.start()
    fetch_help.start()
    for p in range(PHASES):
        lists[PHASES * cap + p] = 0
    for load in loads:
        load.wait()

    def scan(ks, outs, live, base):
        def step(s, carry):
            code = table[ks[s]]
            p = code >> 6
            n = lists[PHASES * cap + p]
            lists[p * cap + n] = ((s + base) << 9) | ((code & 63) << 3) | outs[s]
            lists[PHASES * cap + p] = n + live[s]
            return carry

        lax.fori_loop(0, ks.shape[0], step, 0)

    scan(own_k, own_out, own_live, 0)
    scan(help_k, help_out, help_live, n_own)
    for p in range(PHASES):
        n = lists[PHASES * cap + p]
        for w in range(SCAN):
            lists[p * cap + n + w] = OB
    fetch_own.wait()
    fetch_help.wait()


def pack_kernel(*refs):
    groups, (head, tail) = refs[:NZL], refs[NZL:NZL + 2]
    gone_v, gone_s, sem = refs[NZL + 2:]
    lane = lax.broadcasted_iota(jnp.int32, (8, TILE), 1)
    gone = jnp.zeros((8, TILE), jnp.int32)
    for slot in range(LINE):
        row = groups[slot // NZH][slot % NZH, pl.ds(0, 16), :].astype(jnp.float32)[:1]
        gone = jnp.where((lane == slot) & (row == jnp.inf), 1, gone)
    gone_v[...] = gone
    copy = pltpu.make_async_copy(gone_v, gone_s, sem.at[0])
    copy.start()
    copy.wait()
    lane = lax.broadcasted_iota(jnp.int32, (META, TILE), 1)
    places = jnp.full((META, TILE), ABSENT, jnp.int32)
    n = jnp.int32(0)
    for slot in range(LINE):
        here = gone_s[0, slot] == 0
        tile = groups[slot // NZH].at[slot % NZH]

        @pl.when(here & (n < PACK))
        def _():
            head[pl.ds(pl.multiple_of(n * TILE, TILE), TILE), :] = tile[...]

        @pl.when(here & (n >= PACK))
        def _():
            tail[pl.ds(pl.multiple_of((n - PACK) * TILE, TILE), TILE), :] = tile[...]

        places = jnp.where(lane == slot, jnp.where(here, n, ABSENT), places)
        n = n + jnp.where(here, 1, 0)
    late = (places >= PACK) & (places < ABSENT)
    first = jnp.where(late, LATER, places)
    first = jnp.where(lane == LINE, jnp.where(n > PACK, 1, 0), first)
    second = jnp.where(late, places - PACK, ABSENT)
    second = jnp.where(lane == LINE, 0, second)
    head[pl.ds(PACK * TILE, META), :] = first.astype(jnp.float32).astype(head.dtype)
    tail[pl.ds(REST * TILE, META), :] = second.astype(jnp.float32).astype(tail.dtype)


def pack(groups):
    vmem = pl.BlockSpec(memory_space=pltpu.VMEM)
    return pl.pallas_call(
        pack_kernel,
        out_shape=(
            jax.ShapeDtypeStruct((PACK * TILE + META, TILE), jnp.bfloat16),
            jax.ShapeDtypeStruct((REST * TILE + META, TILE), jnp.bfloat16),
        ),
        in_specs=[vmem] * len(groups),
        out_specs=(vmem, vmem),
        scratch_shapes=[
            pltpu.VMEM((8, TILE), jnp.int32),
            pltpu.SMEM((8, TILE), jnp.int32),
            pltpu.SemaphoreType.DMA((1,)),
        ],
        name="pack",
        compiler_params=pltpu.CompilerParams(vmem_limit_bytes=24 << 20),
    )(*groups)


def task_kernel(phase, places, last, lists_v, tiles, acc_in, over_in, *rest):
    outs, (acc, meta_v, meta_s, lists, picked, sem) = rest[:-6], rest[-6:]
    n_pieces = len(outs) - (3 if last else 2)
    pieces, outs = outs[:n_pieces], outs[n_pieces:]
    cap = tiles.shape[0] + SCAN
    load = pltpu.make_async_copy(lists_v, lists, sem.at[0])
    load.start()
    over = over_in[...]
    for j, piece in enumerate(pieces):
        meta = piece[pl.ds(places * TILE, META), :].astype(jnp.float32).astype(jnp.int32)
        meta_v[pl.ds(j, 1), :] = meta[:1]
        over = over + meta[:8]
    meta_v[pl.ds(n_pieces, 1), :] = over[:1]
    copy = pltpu.make_async_copy(meta_v, meta_s, sem.at[1])
    copy.start()
    acc[pl.ds(0, OB)] = acc_in[...]
    load.wait()
    copy.wait()
    count = lists[PHASES * cap + phase]

    def pick(g, n):
        for u in range(SCAN):
            e = g * SCAN + u
            entry = lists[phase * cap + e]
            place = meta_s[(entry >> 7) & 3, (entry >> 3) & 15]
            picked[n] = (entry & ~120) | ((place & 15) << 3)
            n = n + jnp.where((place < places) & (e < count), 1, 0)
        return n

    n = lax.fori_loop(0, (count + SCAN - 1) >> 3, pick, 0)
    for w in range(WIDE):
        picked[n + w] = OB

    def step(g, carry):
        outputs, prods = [], []
        for w in range(WIDE):
            entry = picked[g * WIDE + w]
            outputs.append(entry & 7)
            rows = pl.ds(pl.multiple_of(((entry >> 3) & 15) * TILE, TILE), TILE)
            a = pieces[0][rows, :]
            for j in range(1, n_pieces):
                a = jnp.where(((entry >> 7) & 3) == j, pieces[j][rows, :], a)
            b = tiles[entry >> 9]
            prods.append(jnp.dot(a, b, preferred_element_type=jnp.float32))
        for w in range(WIDE):
            acc[outputs[w]] += prods[w]
        return carry

    lax.fori_loop(0, (n + WIDE - 1) >> 3, step, 0)
    if last:
        for o in range(OB):
            outs[2][:, o * TILE:(o + 1) * TILE] = acc[o].astype(outs[2].dtype)
    outs[0][...] = acc[pl.ds(0, OB)]
    if last:
        outs[1][0] = meta_s[n_pieces, LINE]
    else:
        outs[1][...] = over


def run_tasks(phase, pieces, acc_in, last, lists, tiles, places=PACK):
    smem = pl.BlockSpec(memory_space=pltpu.SMEM)
    vmem = pl.BlockSpec(memory_space=pltpu.VMEM)
    out_shape = [jax.ShapeDtypeStruct((OB, TILE, TILE), jnp.float32), jax.ShapeDtypeStruct((1,) if last else (8, TILE), jnp.int32)]
    out_specs = [vmem, smem if last else vmem]
    if last:
        out_shape.append(jax.ShapeDtypeStruct((TILE, OB * TILE), jnp.bfloat16))
        out_specs.append(vmem)
    n = tiles.shape[0] * len(pieces) // (NC * NY)
    return pl.pallas_call(
        functools.partial(task_kernel, phase, places, last),
        out_shape=out_shape,
        in_specs=[vmem] * (4 + len(pieces)),
        out_specs=out_specs,
        scratch_shapes=[
            pltpu.VMEM((OB + 1, TILE, TILE), jnp.float32),
            pltpu.VMEM((8, TILE), jnp.int32),
            pltpu.SMEM((8, TILE), jnp.int32),
            pltpu.SMEM(lists.shape, jnp.int32),
            pltpu.SMEM((tiles.shape[0] + 16,), jnp.int32),
            pltpu.SemaphoreType.DMA((2,)),
        ],
        compiler_params=pltpu.CompilerParams(vmem_limit_bytes=24 << 20),
        cost_estimate=pl.CostEstimate(flops=n * 20 * TILE ** 3, bytes_accessed=8 << 20, transcendentals=0),
        name=f"tasks{phase}",
    )(lists, tiles, *acc_in, *pieces)


def prepare(own_tiles, own_k, own_out, own_live, help_tiles, help_k, help_out, help_live):
    me, k = lax.axis_index("col"), jnp.arange(COLS, dtype=jnp.int32)
    c, y = (me ^ k) & 1, (me ^ k) >> 5
    zl, zh = ((me >> 1) - (k >> 1)) & 3, ((me >> 3) - (k >> 3)) & 3
    group = jnp.zeros_like(k)
    for phase, places in enumerate(PLAN):
        for j, (dy, dc) in enumerate(places):
            group = jnp.where((y == dy) & (c == dc), phase * 4 + j, group)
    table = (group * NZL + zl) * NZH + ((zh & 1) << 1 | zh >> 1)
    n = own_k.shape[0] + help_k.shape[0]
    smem = pl.BlockSpec(memory_space=pltpu.SMEM)
    hbm = pl.BlockSpec(memory_space=pltpu.HBM)
    scalars = (own_k, own_out, own_live, help_k, help_out, help_live, table)
    return pl.pallas_call(
        prep_kernel,
        out_shape=(
            jax.ShapeDtypeStruct((PHASES * (n + SCAN) + SCAN,), jnp.int32),
            pltpu.VMEM((n, TILE, TILE), jnp.bfloat16),
        ),
        in_specs=[hbm] * 9,
        out_specs=(smem, pl.BlockSpec(memory_space=pltpu.VMEM)),
        scratch_shapes=[pltpu.SemaphoreType.DMA((2 + len(scalars),))]
        + [pltpu.SMEM(v.shape, jnp.int32) for v in scalars],
        name="prep",
        compiler_params=pltpu.CompilerParams(vmem_limit_bytes=24 << 20),
        cost_estimate=pl.CostEstimate(flops=0, bytes_accessed=8 << 20, transcendentals=0),
    )(*[pltpu.with_memory_space_constraint(v, pltpu.HBM) for v in (*scalars, own_tiles, help_tiles)])


def shards(
    amplitudes,
    amp_kept,
    own_tiles,
    own_k,
    own_out,
    own_live,
    help_tiles,
    help_k,
    help_out,
    help_live,
):
    kept = jnp.where(amp_kept != 0, amplitudes * amp_kept.astype(jnp.bfloat16), jnp.inf).astype(jnp.bfloat16)
    first = jnp.stack([kept] + [move(kept, zh=k) for k in (2, 1, 3)])
    head, tail = pack([first] + [move(first, zl=k) for k in (1, 2, 3)])
    lists, tiles = prepare(
        own_tiles, own_k, own_out, own_live, help_tiles, help_k, help_out, help_live)
    acc = (jnp.zeros((OB, TILE, TILE), jnp.float32), jnp.zeros((8, TILE), jnp.int32))
    ys = {k: move(head, y=k) for k in (2, 1, 3)}
    head_for_c, lists = lax.optimization_barrier((head, lists))
    head_c = move(head_for_c, c=1)
    tasks = functools.partial(run_tasks, lists=lists, tiles=tiles)
    ys[2], own_head = lax.optimization_barrier((ys[2], head))
    y2c = move(ys[2], c=1)
    acc = tasks(0, [own_head, head_c, ys[2]], acc, False)
    ys[1], acc = lax.optimization_barrier((ys[1], acc))
    y1c, y3c = move(ys[1], c=1), move(ys[3], c=1)
    acc = tasks(1, [ys[1], ys[3], y2c], acc, False)
    total, over, out = tasks(2, [y1c, y3c], acc, True)

    def second_round(tail, total, out):
        acc = (total, jnp.zeros((8, TILE), jnp.int32))
        parts = {(k, 0): move(tail, y=k) if k else tail for k in range(NY)}
        parts.update({(k, 1): move(parts[k, 0], c=1) for k in range(NY)})
        for phase, places in enumerate(PLAN):
            acc = tasks(phase, [parts[v] for v in places], acc, phase == 2, places=REST)
        return acc[2]

    return lax.cond(over[0] > 0, second_round, lambda tail, total, out: out, tail, total, out)


def solution(mesh):
    return jax.shard_map(
        shards,
        mesh=mesh,
        in_specs=(
            P("row", "col"),
            P("row", "col"),
            P("col", None, None),
            P("col"),
            P("col"),
            P("col"),
            P("col", None, None),
            P("col"),
            P("col"),
            P("col"),
        ),
        out_specs=P("row", "col"),
        check_vma=False,
    )
```

```python
import functools

import jax
import jax.numpy as jnp
import numpy as np
from jax import lax
from jax.experimental import pallas as pl
from jax.experimental.pallas import tpu as pltpu
from jax.sharding import PartitionSpec as P

TILE = 128
OB = 4
NY, NZH, NZL, NC = 4, 4, 4, 2
COLS = NY * NZH * NZL * NC
LINE = NZH * NZL
PHASES = 3
WIDE = 8
SCAN = 8
PACK = 10
REST = LINE - PACK
META = 16
PLAN = (((0, 0), (0, 1), (2, 0)), ((1, 0), (3, 0), (2, 1)), ((1, 1), (3, 1)))
ABSENT, LATER = 99, 50


def move(x, y=0, zh=0, zl=0, c=0):
    pairs = []
    for i in range(COLS):
        far, near = (i // (NC * NZL) + zh) % NZH, (i // NC + zl) % NZL
        here = ((i // (NC * LINE) ^ y) * NZH + far) * NZL + near
        pairs.append((i, here * NC + (i % NC ^ c)))
    return lax.ppermute(x, "col", pairs)


def prep_kernel(own_k, own_out, own_live, help_k, help_out, help_live, table, own_tiles, help_tiles,
                lists, tiles, sems, *held):
    n_own, n_help = own_k.shape[0], help_k.shape[0]
    cap = n_own + n_help + SCAN
    loads = []
    for j, ref in enumerate((own_k, own_out, own_live, help_k, help_out, help_live, table)):
        loads.append(pltpu.make_async_copy(ref, held[j], sems.at[2 + j]))
        loads[j].start()
    own_k, own_out, own_live, help_k, help_out, help_live, table = held
    fetch_own = pltpu.make_async_copy(own_tiles, tiles.at[pl.ds(0, n_own)], sems.at[0])
    fetch_help = pltpu.make_async_copy(help_tiles, tiles.at[pl.ds(n_own, n_help)], sems.at[1])
    fetch_own.start()
    fetch_help.start()
    for p in range(PHASES):
        lists[PHASES * cap + p] = 0
    for load in loads:
        load.wait()

    def scan(ks, outs, live, base):
        def step(s, carry):
            code = table[ks[s]]
            p = code >> 6
            n = lists[PHASES * cap + p]
            lists[p * cap + n] = ((s + base) << 9) | ((code & 63) << 3) | outs[s]
            lists[PHASES * cap + p] = n + live[s]
            return carry

        lax.fori_loop(0, ks.shape[0], step, 0)

    scan(own_k, own_out, own_live, 0)
    scan(help_k, help_out, help_live, n_own)
    for p in range(PHASES):
        n = lists[PHASES * cap + p]
        for w in range(SCAN):
            lists[p * cap + n + w] = OB
    fetch_own.wait()
    fetch_help.wait()


def pack_kernel(*refs):
    groups, (head, tail) = refs[:NZL], refs[NZL:NZL + 2]
    gone_v, gone_s, sem = refs[NZL + 2:]
    lane = lax.broadcasted_iota(jnp.int32, (8, TILE), 1)
    gone = jnp.zeros((8, TILE), jnp.int32)
    for slot in range(LINE):
        row = groups[slot // NZH][slot % NZH, pl.ds(0, 16), :].astype(jnp.float32)[:1]
        gone = jnp.where((lane == slot) & (row == jnp.inf), 1, gone)
    gone_v[...] = gone
    copy = pltpu.make_async_copy(gone_v, gone_s, sem.at[0])
    copy.start()
    copy.wait()
    lane = lax.broadcasted_iota(jnp.int32, (META, TILE), 1)
    places = jnp.full((META, TILE), ABSENT, jnp.int32)
    n = jnp.int32(0)
    for slot in range(LINE):
        here = gone_s[0, slot] == 0
        tile = groups[slot // NZH].at[slot % NZH]

        @pl.when(here & (n < PACK))
        def _():
            head[pl.ds(pl.multiple_of(n * TILE, TILE), TILE), :] = tile[...]

        @pl.when(here & (n >= PACK))
        def _():
            tail[pl.ds(pl.multiple_of((n - PACK) * TILE, TILE), TILE), :] = tile[...]

        places = jnp.where(lane == slot, jnp.where(here, n, ABSENT), places)
        n = n + jnp.where(here, 1, 0)
    late = (places >= PACK) & (places < ABSENT)
    first = jnp.where(late, LATER, places)
    first = jnp.where(lane == LINE, jnp.where(n > PACK, 1, 0), first)
    second = jnp.where(late, places - PACK, ABSENT)
    second = jnp.where(lane == LINE, 0, second)
    head[pl.ds(PACK * TILE, META), :] = first.astype(jnp.float32).astype(head.dtype)
    tail[pl.ds(REST * TILE, META), :] = second.astype(jnp.float32).astype(tail.dtype)


def pack(groups):
    vmem = pl.BlockSpec(memory_space=pltpu.VMEM)
    return pl.pallas_call(
        pack_kernel,
        out_shape=(
            jax.ShapeDtypeStruct((PACK * TILE + META, TILE), jnp.bfloat16),
            jax.ShapeDtypeStruct((REST * TILE + META, TILE), jnp.bfloat16),
        ),
        in_specs=[vmem] * len(groups),
        out_specs=(vmem, vmem),
        scratch_shapes=[
            pltpu.VMEM((8, TILE), jnp.int32),
            pltpu.SMEM((8, TILE), jnp.int32),
            pltpu.SemaphoreType.DMA((1,)),
        ],
        name="pack",
        compiler_params=pltpu.CompilerParams(vmem_limit_bytes=24 << 20),
    )(*groups)


def task_kernel(phase, places, last, lists_v, tiles, acc_in, over_in, *rest):
    outs, (acc, meta_v, meta_s, lists, picked, sem) = rest[:-6], rest[-6:]
    n_pieces = len(outs) - (3 if last else 2)
    pieces, outs = outs[:n_pieces], outs[n_pieces:]
    cap = tiles.shape[0] + SCAN
    load = pltpu.make_async_copy(lists_v, lists, sem.at[0])
    load.start()
    over = over_in[...]
    for j, piece in enumerate(pieces):
        meta = piece[pl.ds(places * TILE, META), :].astype(jnp.float32).astype(jnp.int32)
        meta_v[pl.ds(j, 1), :] = meta[:1]
        over = over + meta[:8]
    meta_v[pl.ds(n_pieces, 1), :] = over[:1]
    copy = pltpu.make_async_copy(meta_v, meta_s, sem.at[1])
    copy.start()
    acc[pl.ds(0, OB)] = acc_in[...]
    load.wait()
    copy.wait()
    count = lists[PHASES * cap + phase]

    def pick(g, n):
        for u in range(SCAN):
            e = g * SCAN + u
            entry = lists[phase * cap + e]
            place = meta_s[(entry >> 7) & 3, (entry >> 3) & 15]
            picked[n] = (entry & ~120) | ((place & 15) << 3)
            n = n + jnp.where((place < places) & (e < count), 1, 0)
        return n

    n = lax.fori_loop(0, (count + SCAN - 1) >> 3, pick, 0)
    for w in range(WIDE):
        picked[n + w] = OB

    def step(g, carry):
        outputs, prods = [], []
        for w in range(WIDE):
            entry = picked[g * WIDE + w]
            outputs.append(entry & 7)
            rows = pl.ds(pl.multiple_of(((entry >> 3) & 15) * TILE, TILE), TILE)
            a = pieces[0][rows, :]
            for j in range(1, n_pieces):
                a = jnp.where(((entry >> 7) & 3) == j, pieces[j][rows, :], a)
            b = tiles[entry >> 9]
            prods.append(jnp.dot(a, b, preferred_element_type=jnp.float32))
        for w in range(WIDE):
            acc[outputs[w]] += prods[w]
        return carry

    lax.fori_loop(0, (n + WIDE - 1) >> 3, step, 0)
    if last:
        for o in range(OB):
            outs[2][:, o * TILE:(o + 1) * TILE] = acc[o].astype(outs[2].dtype)
    outs[0][...] = acc[pl.ds(0, OB)]
    if last:
        outs[1][0] = meta_s[n_pieces, LINE]
    else:
        outs[1][...] = over


def run_tasks(phase, pieces, acc_in, last, lists, tiles, places=PACK):
    smem = pl.BlockSpec(memory_space=pltpu.SMEM)
    vmem = pl.BlockSpec(memory_space=pltpu.VMEM)
    out_shape = [jax.ShapeDtypeStruct((OB, TILE, TILE), jnp.float32), jax.ShapeDtypeStruct((1,) if last else (8, TILE), jnp.int32)]
    out_specs = [vmem, smem if last else vmem]
    if last:
        out_shape.append(jax.ShapeDtypeStruct((TILE, OB * TILE), jnp.bfloat16))
        out_specs.append(vmem)
    n = tiles.shape[0] * len(pieces) // (NC * NY)
    return pl.pallas_call(
        functools.partial(task_kernel, phase, places, last),
        out_shape=out_shape,
        in_specs=[vmem] * (4 + len(pieces)),
        out_specs=out_specs,
        scratch_shapes=[
            pltpu.VMEM((OB + 1, TILE, TILE), jnp.float32),
            pltpu.VMEM((8, TILE), jnp.int32),
            pltpu.SMEM((8, TILE), jnp.int32),
            pltpu.SMEM(lists.shape, jnp.int32),
            pltpu.SMEM((tiles.shape[0] + 16,), jnp.int32),
            pltpu.SemaphoreType.DMA((2,)),
        ],
        compiler_params=pltpu.CompilerParams(vmem_limit_bytes=24 << 20),
        cost_estimate=pl.CostEstimate(flops=n * 20 * TILE ** 3, bytes_accessed=8 << 20, transcendentals=0),
        name=f"tasks{phase}",
    )(lists, tiles, *acc_in, *pieces)


def prepare(own_tiles, own_k, own_out, own_live, help_tiles, help_k, help_out, help_live):
    me, k = lax.axis_index("col"), jnp.arange(COLS, dtype=jnp.int32)
    c, y = (me ^ k) & 1, (me ^ k) >> 5
    zl, zh = ((me >> 1) - (k >> 1)) & 3, ((me >> 3) - (k >> 3)) & 3
    group = jnp.zeros_like(k)
    for phase, places in enumerate(PLAN):
        for j, (dy, dc) in enumerate(places):
            group = jnp.where((y == dy) & (c == dc), phase * 4 + j, group)
    table = (group * NZL + zl) * NZH + zh
    n = own_k.shape[0] + help_k.shape[0]
    smem = pl.BlockSpec(memory_space=pltpu.SMEM)
    hbm = pl.BlockSpec(memory_space=pltpu.HBM)
    scalars = (own_k, own_out, own_live, help_k, help_out, help_live, table)
    return pl.pallas_call(
        prep_kernel,
        out_shape=(
            jax.ShapeDtypeStruct((PHASES * (n + SCAN) + SCAN,), jnp.int32),
            pltpu.VMEM((n, TILE, TILE), jnp.bfloat16),
        ),
        in_specs=[hbm] * 9,
        out_specs=(smem, pl.BlockSpec(memory_space=pltpu.VMEM)),
        scratch_shapes=[pltpu.SemaphoreType.DMA((2 + len(scalars),))]
        + [pltpu.SMEM(v.shape, jnp.int32) for v in scalars],
        name="prep",
        compiler_params=pltpu.CompilerParams(vmem_limit_bytes=24 << 20),
        cost_estimate=pl.CostEstimate(flops=0, bytes_accessed=8 << 20, transcendentals=0),
    )(*[pltpu.with_memory_space_constraint(v, pltpu.HBM) for v in (*scalars, own_tiles, help_tiles)])


def shards(
    amplitudes,
    amp_kept,
    own_tiles,
    own_k,
    own_out,
    own_live,
    help_tiles,
    help_k,
    help_out,
    help_live,
):
    kept = jnp.where(amp_kept != 0, amplitudes * amp_kept.astype(jnp.bfloat16), jnp.inf).astype(jnp.bfloat16)
    first = jnp.stack([kept] + [move(kept, zh=k) for k in (1, 2, 3)])
    head, tail = pack([first] + [move(first, zl=k) for k in (1, 2, 3)])
    lists, tiles = prepare(
        own_tiles, own_k, own_out, own_live, help_tiles, help_k, help_out, help_live)
    acc = (jnp.zeros((OB, TILE, TILE), jnp.float32), jnp.zeros((8, TILE), jnp.int32))
    ys = {k: move(head, y=k) for k in (2, 1, 3)}
    head_for_c, lists = lax.optimization_barrier((head, lists))
    head_c = move(head_for_c, c=1)
    tasks = functools.partial(run_tasks, lists=lists, tiles=tiles)
    ys[2], own_head = lax.optimization_barrier((ys[2], head))
    y2c = move(ys[2], c=1)
    acc = tasks(0, [own_head, head_c, ys[2]], acc, False)
    ys[1], acc = lax.optimization_barrier((ys[1], acc))
    y1c, y3c = move(ys[1], c=1), move(ys[3], c=1)
    acc = tasks(1, [ys[1], ys[3], y2c], acc, False)
    total, over, out = tasks(2, [y1c, y3c], acc, True)

    def second_round(tail, total, out):
        acc = (total, jnp.zeros((8, TILE), jnp.int32))
        parts = {(k, 0): move(tail, y=k) if k else tail for k in range(NY)}
        parts.update({(k, 1): move(parts[k, 0], c=1) for k in range(NY)})
        for phase, places in enumerate(PLAN):
            acc = tasks(phase, [parts[v] for v in places], acc, phase == 2, places=REST)
        return acc[2]

    return lax.cond(over[0] > 0, second_round, lambda tail, total, out: out, tail, total, out)


def solution(mesh):
    return jax.shard_map(
        shards,
        mesh=mesh,
        in_specs=(
            P("row", "col"),
            P("row", "col"),
            P("col", None, None),
            P("col"),
            P("col"),
            P("col"),
            P("col", None, None),
            P("col"),
            P("col"),
            P("col"),
        ),
        out_specs=P("row", "col"),
        check_vma=False,
    )
```

```python
import functools

import jax
import jax.numpy as jnp
import numpy as np
from jax import lax
from jax.experimental import pallas as pl
from jax.experimental.pallas import tpu as pltpu
from jax.sharding import PartitionSpec as P

TILE = 128
OB = 4
NY, NZH, NZL, NC = 4, 4, 4, 2
COLS = NY * NZH * NZL * NC
LINE = NZH * NZL
PHASES = 3
WIDE = 8
SCAN = 8
PACK = 10
REST = LINE - PACK
META = 16
PLAN = (((0, 0), (2, 0)), ((1, 0), (3, 0), (2, 1), (0, 1)), ((1, 1), (3, 1)))
ABSENT, LATER = 99, 50


def move(x, y=0, zh=0, zl=0, c=0):
    pairs = []
    for i in range(COLS):
        far, near = (i // (NC * NZL) + zh) % NZH, (i // NC + zl) % NZL
        here = ((i // (NC * LINE) ^ y) * NZH + far) * NZL + near
        pairs.append((i, here * NC + (i % NC ^ c)))
    return lax.ppermute(x, "col", pairs)


def prep_kernel(own_k, own_out, own_live, help_k, help_out, help_live, table, own_tiles, help_tiles,
                lists, tiles, sems, *held):
    n_own, n_help = own_k.shape[0], help_k.shape[0]
    cap = n_own + n_help + SCAN
    loads = []
    for j, ref in enumerate((own_k, own_out, own_live, help_k, help_out, help_live, table)):
        loads.append(pltpu.make_async_copy(ref, held[j], sems.at[2 + j]))
        loads[j].start()
    own_k, own_out, own_live, help_k, help_out, help_live, table = held
    fetch_own = pltpu.make_async_copy(own_tiles, tiles.at[pl.ds(0, n_own)], sems.at[0])
    fetch_help = pltpu.make_async_copy(help_tiles, tiles.at[pl.ds(n_own, n_help)], sems.at[1])
    fetch_own.start()
    fetch_help.start()
    for p in range(PHASES):
        lists[PHASES * cap + p] = 0
    for load in loads:
        load.wait()

    def scan(ks, outs, live, base):
        def step(s, carry):
            code = table[ks[s]]
            p = code >> 6
            n = lists[PHASES * cap + p]
            lists[p * cap + n] = ((s + base) << 9) | ((code & 63) << 3) | outs[s]
            lists[PHASES * cap + p] = n + live[s]
            return carry

        lax.fori_loop(0, ks.shape[0], step, 0)

    scan(own_k, own_out, own_live, 0)
    scan(help_k, help_out, help_live, n_own)
    for p in range(PHASES):
        n = lists[PHASES * cap + p]
        for w in range(SCAN):
            lists[p * cap + n + w] = OB
    fetch_own.wait()
    fetch_help.wait()


def pack_kernel(*refs):
    groups, (head, tail) = refs[:NZL], refs[NZL:NZL + 2]
    gone_v, gone_s, sem = refs[NZL + 2:]
    lane = lax.broadcasted_iota(jnp.int32, (8, TILE), 1)
    gone = jnp.zeros((8, TILE), jnp.int32)
    for slot in range(LINE):
        row = groups[slot // NZH][slot % NZH, pl.ds(0, 16), :].astype(jnp.float32)[:1]
        gone = jnp.where((lane == slot) & (row == jnp.inf), 1, gone)
    gone_v[...] = gone
    copy = pltpu.make_async_copy(gone_v, gone_s, sem.at[0])
    copy.start()
    copy.wait()
    lane = lax.broadcasted_iota(jnp.int32, (META, TILE), 1)
    places = jnp.full((META, TILE), ABSENT, jnp.int32)
    n = jnp.int32(0)
    for slot in range(LINE):
        here = gone_s[0, slot] == 0
        tile = groups[slot // NZH].at[slot % NZH]

        @pl.when(here & (n < PACK))
        def _():
            head[pl.ds(pl.multiple_of(n * TILE, TILE), TILE), :] = tile[...]

        @pl.when(here & (n >= PACK))
        def _():
            tail[pl.ds(pl.multiple_of((n - PACK) * TILE, TILE), TILE), :] = tile[...]

        places = jnp.where(lane == slot, jnp.where(here, n, ABSENT), places)
        n = n + jnp.where(here, 1, 0)
    late = (places >= PACK) & (places < ABSENT)
    first = jnp.where(late, LATER, places)
    first = jnp.where(lane == LINE, jnp.where(n > PACK, 1, 0), first)
    second = jnp.where(late, places - PACK, ABSENT)
    second = jnp.where(lane == LINE, 0, second)
    head[pl.ds(PACK * TILE, META), :] = first.astype(jnp.float32).astype(head.dtype)
    tail[pl.ds(REST * TILE, META), :] = second.astype(jnp.float32).astype(tail.dtype)


def pack(groups):
    vmem = pl.BlockSpec(memory_space=pltpu.VMEM)
    return pl.pallas_call(
        pack_kernel,
        out_shape=(
            jax.ShapeDtypeStruct((PACK * TILE + META, TILE), jnp.bfloat16),
            jax.ShapeDtypeStruct((REST * TILE + META, TILE), jnp.bfloat16),
        ),
        in_specs=[vmem] * len(groups),
        out_specs=(vmem, vmem),
        scratch_shapes=[
            pltpu.VMEM((8, TILE), jnp.int32),
            pltpu.SMEM((8, TILE), jnp.int32),
            pltpu.SemaphoreType.DMA((1,)),
        ],
        name="pack",
        compiler_params=pltpu.CompilerParams(vmem_limit_bytes=24 << 20),
    )(*groups)


def task_kernel(phase, places, last, lists_v, tiles, acc_in, over_in, *rest):
    outs, (acc, meta_v, meta_s, lists, picked, sem) = rest[:-6], rest[-6:]
    n_pieces = len(outs) - (3 if last else 2)
    pieces, outs = outs[:n_pieces], outs[n_pieces:]
    cap = tiles.shape[0] + SCAN
    load = pltpu.make_async_copy(lists_v, lists, sem.at[0])
    load.start()
    over = over_in[...]
    for j, piece in enumerate(pieces):
        meta = piece[pl.ds(places * TILE, META), :].astype(jnp.float32).astype(jnp.int32)
        meta_v[pl.ds(j, 1), :] = meta[:1]
        over = over + meta[:8]
    meta_v[pl.ds(n_pieces, 1), :] = over[:1]
    copy = pltpu.make_async_copy(meta_v, meta_s, sem.at[1])
    copy.start()
    acc[pl.ds(0, OB)] = acc_in[...]
    load.wait()
    copy.wait()
    count = lists[PHASES * cap + phase]

    def pick(g, n):
        for u in range(SCAN):
            e = g * SCAN + u
            entry = lists[phase * cap + e]
            place = meta_s[(entry >> 7) & 3, (entry >> 3) & 15]
            picked[n] = (entry & ~120) | ((place & 15) << 3)
            n = n + jnp.where((place < places) & (e < count), 1, 0)
        return n

    n = lax.fori_loop(0, (count + SCAN - 1) >> 3, pick, 0)
    for w in range(WIDE):
        picked[n + w] = OB

    def step(g, carry):
        outputs, prods = [], []
        for w in range(WIDE):
            entry = picked[g * WIDE + w]
            outputs.append(entry & 7)
            rows = pl.ds(pl.multiple_of(((entry >> 3) & 15) * TILE, TILE), TILE)
            a = pieces[0][rows, :]
            for j in range(1, n_pieces):
                a = jnp.where(((entry >> 7) & 3) == j, pieces[j][rows, :], a)
            b = tiles[entry >> 9]
            prods.append(jnp.dot(a, b, preferred_element_type=jnp.float32))
        for w in range(WIDE):
            acc[outputs[w]] += prods[w]
        return carry

    lax.fori_loop(0, (n + WIDE - 1) >> 3, step, 0)
    if last:
        for o in range(OB):
            outs[2][:, o * TILE:(o + 1) * TILE] = acc[o].astype(outs[2].dtype)
    outs[0][...] = acc[pl.ds(0, OB)]
    if last:
        outs[1][0] = meta_s[n_pieces, LINE]
    else:
        outs[1][...] = over


def run_tasks(phase, pieces, acc_in, last, lists, tiles, places=PACK):
    smem = pl.BlockSpec(memory_space=pltpu.SMEM)
    vmem = pl.BlockSpec(memory_space=pltpu.VMEM)
    out_shape = [jax.ShapeDtypeStruct((OB, TILE, TILE), jnp.float32), jax.ShapeDtypeStruct((1,) if last else (8, TILE), jnp.int32)]
    out_specs = [vmem, smem if last else vmem]
    if last:
        out_shape.append(jax.ShapeDtypeStruct((TILE, OB * TILE), jnp.bfloat16))
        out_specs.append(vmem)
    n = tiles.shape[0] * len(pieces) // (NC * NY)
    return pl.pallas_call(
        functools.partial(task_kernel, phase, places, last),
        out_shape=out_shape,
        in_specs=[vmem] * (4 + len(pieces)),
        out_specs=out_specs,
        scratch_shapes=[
            pltpu.VMEM((OB + 1, TILE, TILE), jnp.float32),
            pltpu.VMEM((8, TILE), jnp.int32),
            pltpu.SMEM((8, TILE), jnp.int32),
            pltpu.SMEM(lists.shape, jnp.int32),
            pltpu.SMEM((tiles.shape[0] + 16,), jnp.int32),
            pltpu.SemaphoreType.DMA((2,)),
        ],
        compiler_params=pltpu.CompilerParams(vmem_limit_bytes=24 << 20),
        cost_estimate=pl.CostEstimate(flops=n * 20 * TILE ** 3, bytes_accessed=8 << 20, transcendentals=0),
        name=f"tasks{phase}",
    )(lists, tiles, *acc_in, *pieces)


def prepare(own_tiles, own_k, own_out, own_live, help_tiles, help_k, help_out, help_live):
    me, k = lax.axis_index("col"), jnp.arange(COLS, dtype=jnp.int32)
    c, y = (me ^ k) & 1, (me ^ k) >> 5
    zl, zh = ((me >> 1) - (k >> 1)) & 3, ((me >> 3) - (k >> 3)) & 3
    group = jnp.zeros_like(k)
    for phase, places in enumerate(PLAN):
        for j, (dy, dc) in enumerate(places):
            group = jnp.where((y == dy) & (c == dc), phase * 4 + j, group)
    table = (group * NZL + zl) * NZH + zh
    n = own_k.shape[0] + help_k.shape[0]
    smem = pl.BlockSpec(memory_space=pltpu.SMEM)
    hbm = pl.BlockSpec(memory_space=pltpu.HBM)
    scalars = (own_k, own_out, own_live, help_k, help_out, help_live, table)
    return pl.pallas_call(
        prep_kernel,
        out_shape=(
            jax.ShapeDtypeStruct((PHASES * (n + SCAN) + SCAN,), jnp.int32),
            pltpu.VMEM((n, TILE, TILE), jnp.bfloat16),
        ),
        in_specs=[hbm] * 9,
        out_specs=(smem, pl.BlockSpec(memory_space=pltpu.VMEM)),
        scratch_shapes=[pltpu.SemaphoreType.DMA((2 + len(scalars),))]
        + [pltpu.SMEM(v.shape, jnp.int32) for v in scalars],
        name="prep",
        compiler_params=pltpu.CompilerParams(vmem_limit_bytes=24 << 20),
        cost_estimate=pl.CostEstimate(flops=0, bytes_accessed=8 << 20, transcendentals=0),
    )(*[pltpu.with_memory_space_constraint(v, pltpu.HBM) for v in (*scalars, own_tiles, help_tiles)])


def shards(
    amplitudes,
    amp_kept,
    own_tiles,
    own_k,
    own_out,
    own_live,
    help_tiles,
    help_k,
    help_out,
    help_live,
):
    kept = jnp.where(amp_kept != 0, amplitudes * amp_kept.astype(jnp.bfloat16), jnp.inf).astype(jnp.bfloat16)
    first = jnp.stack([kept] + [move(kept, zh=k) for k in (1, 2, 3)])
    near = [first] + [move(first, zl=k) for k in (1, 2, 3)]
    lists, tiles = prepare(
        own_tiles, own_k, own_out, own_live, help_tiles, help_k, help_out, help_live)
    near[3], lists = lax.optimization_barrier((near[3], lists))
    head, tail = pack(near)
    acc = (jnp.zeros((OB, TILE, TILE), jnp.float32), jnp.zeros((8, TILE), jnp.int32))
    ys = {k: move(head, y=k) for k in (2, 1, 3)}
    head_c = move(head, c=1)
    tasks = functools.partial(run_tasks, lists=lists, tiles=tiles)
    ys[2], own_head = lax.optimization_barrier((ys[2], head))
    y2c = move(ys[2], c=1)
    acc = tasks(0, [own_head, ys[2]], acc, False)
    ys[1], acc = lax.optimization_barrier((ys[1], acc))
    y1c, y3c = move(ys[1], c=1), move(ys[3], c=1)
    acc = tasks(1, [ys[1], ys[3], y2c, head_c], acc, False)
    total, over, out = tasks(2, [y1c, y3c], acc, True)

    def second_round(tail, total, out):
        acc = (total, jnp.zeros((8, TILE), jnp.int32))
        parts = {(k, 0): move(tail, y=k) if k else tail for k in range(NY)}
        parts.update({(k, 1): move(parts[k, 0], c=1) for k in range(NY)})
        for phase, places in enumerate(PLAN):
            acc = tasks(phase, [parts[v] for v in places], acc, phase == 2, places=REST)
        return acc[2]

    return lax.cond(over[0] > 0, second_round, lambda tail, total, out: out, tail, total, out)


def solution(mesh):
    return jax.shard_map(
        shards,
        mesh=mesh,
        in_specs=(
            P("row", "col"),
            P("row", "col"),
            P("col", None, None),
            P("col"),
            P("col"),
            P("col"),
            P("col", None, None),
            P("col"),
            P("col"),
            P("col"),
        ),
        out_specs=P("row", "col"),
        check_vma=False,
    )
```

```python
import functools

import jax
import jax.numpy as jnp
import numpy as np
from jax import lax
from jax.experimental import pallas as pl
from jax.experimental.pallas import tpu as pltpu
from jax.sharding import PartitionSpec as P

TILE = 128
OB = 4
NY, NZH, NZL, NC = 4, 4, 4, 2
COLS = NY * NZH * NZL * NC
LINE = NZH * NZL
PHASES = 3
WIDE = 8
SCAN = 8
PACK = 10
REST = LINE - PACK
META = 16
PLAN = (((0, 0), (0, 1), (2, 0)), ((1, 0), (3, 0), (2, 1)), ((1, 1), (3, 1)))
ABSENT, LATER = 99, 50


def move(x, y=0, zh=0, zl=0, c=0):
    pairs = []
    for i in range(COLS):
        far, near = (i // (NC * NZL) + zh) % NZH, (i // NC + zl) % NZL
        here = ((i // (NC * LINE) ^ y) * NZH + far) * NZL + near
        pairs.append((i, here * NC + (i % NC ^ c)))
    return lax.ppermute(x, "col", pairs)


def prep_kernel(own_k, own_out, own_live, help_k, help_out, help_live, table, own_tiles, help_tiles,
                lists, tiles, sems, *held):
    n_own, n_help = own_k.shape[0], help_k.shape[0]
    cap = n_own + n_help + SCAN
    loads = []
    for j, ref in enumerate((own_k, own_out, own_live, help_k, help_out, help_live, table)):
        loads.append(pltpu.make_async_copy(ref, held[j], sems.at[2 + j]))
        loads[j].start()
    own_k, own_out, own_live, help_k, help_out, help_live, table = held
    fetch_own = pltpu.make_async_copy(own_tiles, tiles.at[pl.ds(0, n_own)], sems.at[0])
    fetch_help = pltpu.make_async_copy(help_tiles, tiles.at[pl.ds(n_own, n_help)], sems.at[1])
    fetch_own.start()
    fetch_help.start()
    for p in range(PHASES):
        lists[PHASES * cap + p] = 0
    for load in loads:
        load.wait()

    def scan(ks, outs, live, base):
        def step(s, carry):
            code = table[ks[s]]
            p = code >> 6
            n = lists[PHASES * cap + p]
            lists[p * cap + n] = ((s + base) << 9) | ((code & 63) << 3) | outs[s]
            lists[PHASES * cap + p] = n + live[s]
            return carry

        lax.fori_loop(0, ks.shape[0], step, 0)

    scan(own_k, own_out, own_live, 0)
    scan(help_k, help_out, help_live, n_own)
    for p in range(PHASES):
        n = lists[PHASES * cap + p]
        for w in range(SCAN):
            lists[p * cap + n + w] = OB
    fetch_own.wait()
    fetch_help.wait()


def pack_kernel(*refs):
    groups, (head, tail) = refs[:NZL], refs[NZL:NZL + 2]
    gone_v, gone_s, sem = refs[NZL + 2:]
    lane = lax.broadcasted_iota(jnp.int32, (8, TILE), 1)
    gone = jnp.zeros((8, TILE), jnp.int32)
    for slot in range(LINE):
        row = groups[slot // NZH][slot % NZH, pl.ds(0, 16), :].astype(jnp.float32)[:1]
        gone = jnp.where((lane == slot) & (row == jnp.inf), 1, gone)
    gone_v[...] = gone
    copy = pltpu.make_async_copy(gone_v, gone_s, sem.at[0])
    copy.start()
    copy.wait()
    lane = lax.broadcasted_iota(jnp.int32, (META, TILE), 1)
    places = jnp.full((META, TILE), ABSENT, jnp.int32)
    n = jnp.int32(0)
    for slot in range(LINE):
        here = gone_s[0, slot] == 0
        tile = groups[slot // NZH].at[slot % NZH]

        @pl.when(here & (n < PACK))
        def _():
            head[pl.ds(pl.multiple_of(n * TILE, TILE), TILE), :] = tile[...]

        @pl.when(here & (n >= PACK))
        def _():
            tail[pl.ds(pl.multiple_of((n - PACK) * TILE, TILE), TILE), :] = tile[...]

        places = jnp.where(lane == slot, jnp.where(here, n, ABSENT), places)
        n = n + jnp.where(here, 1, 0)
    late = (places >= PACK) & (places < ABSENT)
    first = jnp.where(late, LATER, places)
    first = jnp.where(lane == LINE, jnp.where(n > PACK, 1, 0), first)
    second = jnp.where(late, places - PACK, ABSENT)
    second = jnp.where(lane == LINE, 0, second)
    head[pl.ds(PACK * TILE, META), :] = first.astype(jnp.float32).astype(head.dtype)
    tail[pl.ds(REST * TILE, META), :] = second.astype(jnp.float32).astype(tail.dtype)


def pack(groups):
    vmem = pl.BlockSpec(memory_space=pltpu.VMEM)
    return pl.pallas_call(
        pack_kernel,
        out_shape=(
            jax.ShapeDtypeStruct((PACK * TILE + META, TILE), jnp.bfloat16),
            jax.ShapeDtypeStruct((REST * TILE + META, TILE), jnp.bfloat16),
        ),
        in_specs=[vmem] * len(groups),
        out_specs=(vmem, vmem),
        scratch_shapes=[
            pltpu.VMEM((8, TILE), jnp.int32),
            pltpu.SMEM((8, TILE), jnp.int32),
            pltpu.SemaphoreType.DMA((1,)),
        ],
        name="pack",
        compiler_params=pltpu.CompilerParams(vmem_limit_bytes=24 << 20),
    )(*groups)


def task_kernel(phase, places, last, lists_v, tiles, acc_in, over_in, *rest):
    outs, (acc, meta_v, meta_s, lists, picked, sem) = rest[:-6], rest[-6:]
    n_pieces = len(outs) - (3 if last else 2)
    pieces, outs = outs[:n_pieces], outs[n_pieces:]
    cap = tiles.shape[0] + SCAN
    load = pltpu.make_async_copy(lists_v, lists, sem.at[0])
    load.start()
    over = over_in[...]
    for j, piece in enumerate(pieces):
        meta = piece[pl.ds(places * TILE, META), :].astype(jnp.float32).astype(jnp.int32)
        meta_v[pl.ds(j, 1), :] = meta[:1]
        over = over + meta[:8]
    meta_v[pl.ds(n_pieces, 1), :] = over[:1]
    copy = pltpu.make_async_copy(meta_v, meta_s, sem.at[1])
    copy.start()
    acc[pl.ds(0, OB)] = acc_in[...]
    load.wait()
    copy.wait()
    count = lists[PHASES * cap + phase]

    def pick(g, n):
        for u in range(SCAN):
            e = g * SCAN + u
            entry = lists[phase * cap + e]
            place = meta_s[(entry >> 7) & 3, (entry >> 3) & 15]
            picked[n] = (entry & ~120) | ((place & 15) << 3)
            n = n + jnp.where((place < places) & (e < count), 1, 0)
        return n

    n = lax.fori_loop(0, (count + SCAN - 1) >> 3, pick, 0)
    for w in range(WIDE):
        picked[n + w] = OB

    def step(g, carry):
        outputs, prods = [], []
        for w in range(WIDE):
            entry = picked[g * WIDE + w]
            outputs.append(entry & 7)
            rows = pl.ds(pl.multiple_of(((entry >> 3) & 15) * TILE, TILE), TILE)
            a = pieces[0][rows, :]
            for j in range(1, n_pieces):
                a = jnp.where(((entry >> 7) & 3) == j, pieces[j][rows, :], a)
            b = tiles[entry >> 9]
            prods.append(jnp.dot(a, b, preferred_element_type=jnp.float32))
        for w in range(WIDE):
            acc[outputs[w]] += prods[w]
        return carry

    lax.fori_loop(0, (n + WIDE - 1) >> 3, step, 0)
    if last:
        for o in range(OB):
            outs[2][:, o * TILE:(o + 1) * TILE] = acc[o].astype(outs[2].dtype)
    outs[0][...] = acc[pl.ds(0, OB)]
    if last:
        outs[1][0] = meta_s[n_pieces, LINE]
    else:
        outs[1][...] = over


def run_tasks(phase, pieces, acc_in, last, lists, tiles, places=PACK):
    smem = pl.BlockSpec(memory_space=pltpu.SMEM)
    vmem = pl.BlockSpec(memory_space=pltpu.VMEM)
    out_shape = [jax.ShapeDtypeStruct((OB, TILE, TILE), jnp.float32), jax.ShapeDtypeStruct((1,) if last else (8, TILE), jnp.int32)]
    out_specs = [vmem, smem if last else vmem]
    if last:
        out_shape.append(jax.ShapeDtypeStruct((TILE, OB * TILE), jnp.bfloat16))
        out_specs.append(vmem)
    n = tiles.shape[0] * len(pieces) // (NC * NY)
    return pl.pallas_call(
        functools.partial(task_kernel, phase, places, last),
        out_shape=out_shape,
        in_specs=[vmem] * (4 + len(pieces)),
        out_specs=out_specs,
        scratch_shapes=[
            pltpu.VMEM((OB + 1, TILE, TILE), jnp.float32),
            pltpu.VMEM((8, TILE), jnp.int32),
            pltpu.SMEM((8, TILE), jnp.int32),
            pltpu.SMEM(lists.shape, jnp.int32),
            pltpu.SMEM((tiles.shape[0] + 16,), jnp.int32),
            pltpu.SemaphoreType.DMA((2,)),
        ],
        compiler_params=pltpu.CompilerParams(vmem_limit_bytes=24 << 20),
        cost_estimate=pl.CostEstimate(flops=n * 20 * TILE ** 3, bytes_accessed=8 << 20, transcendentals=0),
        name=f"tasks{phase}",
    )(lists, tiles, *acc_in, *pieces)


def prepare(own_tiles, own_k, own_out, own_live, help_tiles, help_k, help_out, help_live):
    me, k = lax.axis_index("col"), jnp.arange(COLS, dtype=jnp.int32)
    c, y = (me ^ k) & 1, (me ^ k) >> 5
    zl, zh = ((me >> 1) - (k >> 1)) & 3, ((me >> 3) - (k >> 3)) & 3
    group = jnp.zeros_like(k)
    for phase, places in enumerate(PLAN):
        for j, (dy, dc) in enumerate(places):
            group = jnp.where((y == dy) & (c == dc), phase * 4 + j, group)
    table = (group * NZL + zl) * NZH + (zh ^ (zh >> 1))
    n = own_k.shape[0] + help_k.shape[0]
    smem = pl.BlockSpec(memory_space=pltpu.SMEM)
    hbm = pl.BlockSpec(memory_space=pltpu.HBM)
    scalars = (own_k, own_out, own_live, help_k, help_out, help_live, table)
    return pl.pallas_call(
        prep_kernel,
        out_shape=(
            jax.ShapeDtypeStruct((PHASES * (n + SCAN) + SCAN,), jnp.int32),
            pltpu.VMEM((n, TILE, TILE), jnp.bfloat16),
        ),
        in_specs=[hbm] * 9,
        out_specs=(smem, pl.BlockSpec(memory_space=pltpu.VMEM)),
        scratch_shapes=[pltpu.SemaphoreType.DMA((2 + len(scalars),))]
        + [pltpu.SMEM(v.shape, jnp.int32) for v in scalars],
        name="prep",
        compiler_params=pltpu.CompilerParams(vmem_limit_bytes=24 << 20),
        cost_estimate=pl.CostEstimate(flops=0, bytes_accessed=8 << 20, transcendentals=0),
    )(*[pltpu.with_memory_space_constraint(v, pltpu.HBM) for v in (*scalars, own_tiles, help_tiles)])


def shards(
    amplitudes,
    amp_kept,
    own_tiles,
    own_k,
    own_out,
    own_live,
    help_tiles,
    help_k,
    help_out,
    help_live,
):
    kept = jnp.where(amp_kept != 0, amplitudes * amp_kept.astype(jnp.bfloat16), jnp.inf).astype(jnp.bfloat16)
    first = jnp.stack([kept] + [move(kept, zh=k) for k in (1, 3, 2)])
    head, tail = pack([first] + [move(first, zl=k) for k in (1, 2, 3)])
    lists, tiles = prepare(
        own_tiles, own_k, own_out, own_live, help_tiles, help_k, help_out, help_live)
    acc = (jnp.zeros((OB, TILE, TILE), jnp.float32), jnp.zeros((8, TILE), jnp.int32))
    ys = {k: move(head, y=k) for k in (2, 1, 3)}
    head_for_c, lists = lax.optimization_barrier((head, lists))
    head_c = move(head_for_c, c=1)
    tasks = functools.partial(run_tasks, lists=lists, tiles=tiles)
    ys[2], own_head = lax.optimization_barrier((ys[2], head))
    y2c = move(ys[2], c=1)
    acc = tasks(0, [own_head, head_c, ys[2]], acc, False)
    ys[1], acc = lax.optimization_barrier((ys[1], acc))
    y1c, y3c = move(ys[1], c=1), move(ys[3], c=1)
    acc = tasks(1, [ys[1], ys[3], y2c], acc, False)
    total, over, out = tasks(2, [y1c, y3c], acc, True)

    def second_round(tail, total, out):
        acc = (total, jnp.zeros((8, TILE), jnp.int32))
        parts = {(k, 0): move(tail, y=k) if k else tail for k in range(NY)}
        parts.update({(k, 1): move(parts[k, 0], c=1) for k in range(NY)})
        for phase, places in enumerate(PLAN):
            acc = tasks(phase, [parts[v] for v in places], acc, phase == 2, places=REST)
        return acc[2]

    return lax.cond(over[0] > 0, second_round, lambda tail, total, out: out, tail, total, out)


def solution(mesh):
    return jax.shard_map(
        shards,
        mesh=mesh,
        in_specs=(
            P("row", "col"),
            P("row", "col"),
            P("col", None, None),
            P("col"),
            P("col"),
            P("col"),
            P("col", None, None),
            P("col"),
            P("col"),
            P("col"),
        ),
        out_specs=P("row", "col"),
        check_vma=False,
    )
```
